256 devices in a mesh: dp: 16 (over z, y_hi), tensor: 16 (over x, y_lo, core).
Axes of the slice: x: 4, y: 4 (y_hi: 2, y_lo: 2; y = y_hi * 2 + y_lo), z: 8, core: 2. Of those that a mesh axis runs over, the one named last changes fastest.
Arguments:
- tokens: bfloat16 [8192, 16384], P('dp', 'tensor'), may hold values from -6 to 6
- queries: bfloat16 [8192, 16384], P('dp', 'tensor'), as said below
- out_grad: bfloat16 [8192, 16384], P('dp', 'tensor'), may hold values from -6 to 6
- key_weight: bfloat16 [16384, 1024], P('tensor'), may hold values from -0.0625 to 0.0625
- value_weight: bfloat16 [16384, 1024], P('tensor'), may hold values from -0.0625 to 0.0625
- key_scale: float32 [32, 1024], replicated, may hold values from 0.1 to 1.9
- value_scale: float32 [32, 1024], replicated, may hold values from 0.1 to 1.9
- segment_ids: int32 [16, 512], P('dp'), may hold values from 0 to 3, never falling along the last dimension, each value on 1 to 256 neighbouring positions
- tenant_ids: int32 [16, 4], P('dp'), may hold values from 0 to 31
Outputs:
- input_grad: bfloat16 [8192, 16384], P('dp', 'tensor')
- key_scale_grad: float32 [32, 1024], P(None, 'tensor')
- value_scale_grad: float32 [32, 1024], P(None, 'tensor')
The draws below stay inside these ranges and needn't reach their ends.
Inputs may be any that keep to these rules, and one draw needn't show every extreme that they name: `segment_ids`: in each token group the sequence number never falls, all 4 sequences are present, and the longest holds exactly 256 tokens. `queries`: entries lie between -160 and 160.
All inputs are finite; a program needn't handle non-finite values.
Results may differ from the reference program's by a relative error of at most 0.034.
The reference program's roundings to bfloat16 on the way count: a program that leaves them out, or rounds other values in their place, can miss the bound.
Values may be sent and summed in bfloat16 or wider, within the bound.
No kernel may reach another device: no remote copies, remote signals or barrier semaphores. Data moves between devices by JAX's collectives and lax.ppermute only.
A program may use at most 128 MiB of HBM per device.

```python
import math
import jax
import jax.numpy as jnp
import numpy as np
from jax import lax

D = 16384
HD = 128
GROUP = 16
HQ = 128
KV = 8
TOK = 512
SEQS = 4
NT = 32
GROUPS = 16
TOKENS = 8192


def draw_queries(key, part):
    key = jax.random.fold_in(key, 7)
    normal_key = jax.random.fold_in(key, 0)
    values_drawn = jax.random.normal(normal_key, (TOKENS, HQ * HD), jnp.float32)
    values_drawn = jnp.clip(values_drawn, -6.0, 6.0)
    return values_drawn.astype(jnp.bfloat16)


def plant(array, key, low, high):
    longest = array.shape.index(max(array.shape))
    spots = []
    for shift in (0, 1):
        where = [jax.random.randint(jax.random.fold_in(key, axis), (), 0, length) for axis, length in enumerate(array.shape)]
        where[longest] = (where[longest] + shift) % array.shape[longest]
        spots.append(tuple(where))
    return array.at[spots[0]].set(low).at[spots[1]].set(high)


def with_spikes(result, own_key, source, target, blocks, factor):
    def block_of(dim):
        return (jnp.arange(result.shape[dim]) // (result.shape[dim] // blocks)).reshape((-1,) + (1,) * (result.ndim - 1 - dim))

    one_side = jax.random.permutation(own_key, blocks)[block_of(target)]
    other_side = (block_of(target) + blocks // 2) % blocks
    return jnp.where((block_of(source) == one_side) | (block_of(source) == other_side), factor * result, result)


def shard_levels(own_key, dims, pieces, least, high):
    level, own = 1.0, jax.random.fold_in(own_key, 6)
    for dim, parts in pieces:
        heights = jnp.exp(jax.random.uniform(jax.random.fold_in(own, dim), (parts,), jnp.float32, least / len(pieces), high / len(pieces)))
        level = level * jnp.repeat(heights, dims[dim] // parts).reshape([-1 if axis == dim else 1 for axis in range(len(dims))])
    return level


def split_up(amount, total, limit, skew):
    weights = [(1 << 20) // math.isqrt(rank ** skew) + 1 for rank in range(2, amount + 1)]
    rest, given = total - limit - (amount - 1), [1] * (amount - 1)
    while rest > 0:
        movable = [i for i in range(amount - 1) if given[i] < limit]
        pool, left = sum([weights[i] for i in movable]), rest
        for i in movable:
            extra = min(limit - given[i], max(1, left * weights[i] // pool), rest)
            given[i] = given[i] + extra
            rest = rest - extra
    return np.array([limit] + given)


def uneven(rng, number_of, total, bound, slope):
    if number_of == 2:
        one = jax.random.randint(rng, (), max(1, total - bound), min(bound, total - 1) + 1)
        return jnp.stack([one, total - one])
    sizes = jnp.asarray(split_up(number_of, total, bound, slope), jnp.int32)
    twos = (number_of - 1) // 2
    donor, receiver = sizes[1:1 + 2 * twos:2], sizes[2:2 + 2 * twos:2]
    slack = jnp.minimum(donor - 1, bound - receiver)
    passed = jax.random.randint(jax.random.fold_in(rng, 1), (twos,), 0, 1 << 20) % (slack + 1)
    sizes = sizes.at[1:1 + 2 * twos:2].set(donor - passed).at[2:2 + 2 * twos:2].set(receiver + passed)
    return sizes[jax.random.permutation(jax.random.fold_in(rng, 2), number_of)]


def scatter_about(own_key, dims, deviation, bound, cuts=(), kind=jnp.bfloat16):
    drawn = deviation * jax.random.normal(own_key, dims, jnp.float32)
    if cuts:
        drawn = drawn * shard_levels(own_key, dims, cuts, -0.22, 0.18)
    return jnp.clip(drawn, -bound, bound).astype(kind)


def noise_with(own_key, extent, spread, most, pieces, heavy, kind=jnp.bfloat16):
    drawn = spread * jax.random.normal(own_key, extent, jnp.float32)
    if pieces:
        drawn = drawn * shard_levels(own_key, extent, pieces, -0.22, 0.18)
    return jnp.clip(with_spikes(drawn, jax.random.fold_in(own_key, 3), *heavy), -most, most).astype(kind)


def setup_inputs(seed: int = 0) -> dict:
    seeds = jax.random.split(jax.random.key(seed), 10)
    tokens = scatter_about(seeds[0], (TOKENS, D), 1.0, 6.0, ((0, 16), (1, 16)))
    queries = draw_queries(jax.random.fold_in(seeds[9], 71), 0)
    out_grad = scatter_about(seeds[2], (TOKENS, HQ * HD), 1.0, 6.0, ((0, 16), (1, 16)))
    key_weight = noise_with(seeds[3], (D, KV * HD), D ** -0.5, 0.0625, ((0, 16),), (0, 1, 16, 2.0))
    value_weight = noise_with(seeds[4], (D, KV * HD), D ** -0.5, 0.0625, ((0, 16),), (0, 1, 16, 2.0))
    key_scale = jnp.clip(1.0 + 0.18 * jax.random.normal(seeds[5], (NT, KV * HD), jnp.float32), 0.1, 1.9)
    value_scale = jnp.clip(1.0 + 0.18 * jax.random.normal(seeds[6], (NT, KV * HD), jnp.float32), 0.1, 1.9)
    segment_ids = jax.vmap(lambda own: jnp.searchsorted(jnp.cumsum(uneven(own, SEQS, TOK, TOK // 2, 0)), jnp.arange(TOK), side="right"))(jax.random.split(seeds[7], GROUPS)).reshape((GROUPS, TOK)).astype(jnp.int32)
    tenant_ids = plant(jax.random.randint(seeds[8], (GROUPS, SEQS), 0, NT), jax.random.fold_in(seeds[8], 1), 0, NT - 1).astype(jnp.int32)
    return dict(tokens=tokens, queries=queries, out_grad=out_grad, key_weight=key_weight, value_weight=value_weight, key_scale=key_scale, value_scale=value_scale, segment_ids=segment_ids, tenant_ids=tenant_ids)


def tenant_rows(segments, tenants):
    seq_match = segments[:, None] == jnp.arange(SEQS, dtype=jnp.int32)[None, :]
    tenant_tok = jnp.sum(jnp.where(seq_match, tenants[None, :], 0), axis=1).astype(jnp.int32)
    return (tenant_tok[:, None] == jnp.arange(NT, dtype=jnp.int32)[None, :]).astype(jnp.float32)


def allowed_mask(segments):
    position = jnp.arange(segments.shape[0], dtype=jnp.int32)
    return (segments[:, None] == segments[None, :]) & (position[None, :] <= position[:, None])


def head_grads(query_head, out_head, key_tile, value_tile, allowed):
    score_scale = HD ** -0.5
    scores = lax.dot_general(query_head, key_tile, (((1,), (1,)), ((), ())), preferred_element_type=jnp.float32) * score_scale
    scores = jnp.where(allowed, scores, -1e30)
    row_peak = jnp.max(scores, axis=1, keepdims=True)
    exp_scores = jnp.exp(scores - row_peak)
    probs = exp_scores / jnp.sum(exp_scores, axis=1, keepdims=True)
    probs_low = probs.astype(jnp.bfloat16)
    attended = jnp.dot(probs_low, value_tile, preferred_element_type=jnp.float32)
    row_delta = jnp.sum(out_head.astype(jnp.float32) * attended, axis=1, keepdims=True)
    prob_grad = lax.dot_general(out_head, value_tile, (((1,), (1,)), ((), ())), preferred_element_type=jnp.float32)
    score_grad = (probs * (prob_grad - row_delta)).astype(jnp.bfloat16)
    value_grad = lax.dot_general(probs_low, out_head, (((0,), (0,)), ((), ())), preferred_element_type=jnp.float32)
    key_grad = lax.dot_general(score_grad, query_head, (((0,), (0,)), ((), ())), preferred_element_type=jnp.float32) * score_scale
    return key_grad, value_grad


def group_grads(group_tokens, group_queries, group_outs, segments, tenants, key_weight, value_weight, key_scale, value_scale):
    tenant_hot = tenant_rows(segments, tenants)
    key_base = jnp.dot(group_tokens, key_weight, preferred_element_type=jnp.float32)
    value_base = jnp.dot(group_tokens, value_weight, preferred_element_type=jnp.float32)
    key_factor = jnp.dot(tenant_hot, key_scale, precision=lax.Precision.HIGHEST)
    value_factor = jnp.dot(tenant_hot, value_scale, precision=lax.Precision.HIGHEST)
    key_all = (key_base * key_factor).astype(jnp.bfloat16)
    value_all = (value_base * value_factor).astype(jnp.bfloat16)
    allowed = allowed_mask(segments)

    def one_kv(kv_index):
        key_tile = lax.dynamic_slice_in_dim(key_all, kv_index * HD, HD, 1)
        value_tile = lax.dynamic_slice_in_dim(value_all, kv_index * HD, HD, 1)

        def one_query(totals, query_index):
            column = ((kv_index * GROUP + query_index) * HD).astype(jnp.int32)
            query_head = lax.dynamic_slice_in_dim(group_queries, column, HD, 1)
            out_head = lax.dynamic_slice_in_dim(group_outs, column, HD, 1)
            key_part, value_part = head_grads(query_head, out_head, key_tile, value_tile, allowed)
            return (totals[0] + key_part, totals[1] + value_part), None

        zeros_tile = jnp.zeros((TOK, HD), jnp.float32)
        sums_out, unused = lax.scan(one_query, (zeros_tile, zeros_tile), jnp.arange(GROUP, dtype=jnp.int32))
        return sums_out

    key_heads, value_heads = lax.map(one_kv, jnp.arange(KV, dtype=jnp.int32))
    key_grad = jnp.transpose(key_heads, (1, 0, 2)).reshape(TOK, KV * HD)
    value_grad = jnp.transpose(value_heads, (1, 0, 2)).reshape(TOK, KV * HD)
    key_low = (key_grad * key_factor).astype(jnp.bfloat16)
    value_low = (value_grad * value_factor).astype(jnp.bfloat16)
    input_grad = lax.dot_general(key_low, key_weight, (((1,), (1,)), ((), ())), preferred_element_type=jnp.float32)
    input_grad = input_grad + lax.dot_general(value_low, value_weight, (((1,), (1,)), ((), ())), preferred_element_type=jnp.float32)
    key_tenant = lax.dot_general(tenant_hot, key_grad * key_base, (((0,), (0,)), ((), ())), precision=lax.Precision.HIGHEST)
    value_tenant = lax.dot_general(tenant_hot, value_grad * value_base, (((0,), (0,)), ((), ())), precision=lax.Precision.HIGHEST)
    return input_grad.astype(jnp.bfloat16), key_tenant, value_tenant


def reference(tokens, queries, out_grad, key_weight, value_weight, key_scale, value_scale, segment_ids, tenant_ids):
    grouped_tokens = tokens.reshape(GROUPS, TOK, D)
    grouped_queries = queries.reshape(GROUPS, TOK, HQ * HD)
    grouped_outs = out_grad.reshape(GROUPS, TOK, HQ * HD)

    def step_group(totals, inputs):
        group_tokens, group_queries, group_outs, segments, tenants = inputs
        input_grad, key_tenant, value_tenant = group_grads(group_tokens, group_queries, group_outs, segments, tenants, key_weight, value_weight, key_scale, value_scale)
        return (totals[0] + key_tenant, totals[1] + value_tenant), input_grad

    zeros_table = jnp.zeros((NT, KV * HD), jnp.float32)
    sums_out, grads_out = lax.scan(step_group, (zeros_table, zeros_table), (grouped_tokens, grouped_queries, grouped_outs, segment_ids, tenant_ids))
    return grads_out.reshape(TOKENS, D), sums_out[0], sums_out[1]
```

```python
import functools

import jax
import jax.numpy as jnp
from jax import lax
from jax.experimental import pallas as pl
from jax.experimental.pallas import tpu as pltpu
from jax.sharding import PartitionSpec as P

SEQS = 4
NT = 32
HEAD = 128
TOK = 512
HALF = 256
CHIPS = 8
BLOCK = 128
LOG2E = 1.4426950408889634
SCALE = HEAD**-0.5
BF = jnp.bfloat16
F32 = jnp.float32
VMEM_BYTES = 48 * 1024 * 1024


def params():
    return pltpu.CompilerParams(vmem_limit_bytes=VMEM_BYTES)


def device_index(x, y, core):
    return (x % 4 * 2 + y) * 2 + core


def tensor_pairs(step):
    places = [(x, y, core) for x in range(4) for y in range(2) for core in range(2)]
    return [(device_index(*place), device_index(*step(*place))) for place in places]


CORE_SWAP = tensor_pairs(lambda x, y, core: (x, y, core ^ 1))
SAME_CORE = [[chip * 2 + core for chip in range(CHIPS)] for core in range(2)]


def project_body(place, tok_send, tok_keep, kw, vw, send, keep, rows):
    @pl.when(pl.program_id(0) == 0)
    def _():
        rows[:HALF] = tok_send[...]
        rows[HALF:] = tok_keep[...]

    for part, weight in enumerate((kw, vw)):
        total = jnp.dot(rows[...], weight[...], preferred_element_type=F32)
        for head in range(2):
            block = total[:, head * HEAD : (head + 1) * HEAD]
            columns = slice(part * HEAD, (part + 1) * HEAD)
            send[head, :, columns] = block[:HALF]
            keep[head, :, columns] = block[HALF:]


def project(place, tokens, key_weight, value_weight):
    depth = tokens.shape[1]
    out = jax.ShapeDtypeStruct((CHIPS, HALF, 2 * HEAD), F32)
    return pl.pallas_call(
        project_body,
        grid_spec=pltpu.PrefetchScalarGridSpec(
            num_scalar_prefetch=1,
            grid=(CHIPS // 2,),
            in_specs=[
                pl.BlockSpec((HALF, depth), lambda i, place: (1 - place[0], 0)),
                pl.BlockSpec((HALF, depth), lambda i, place: (place[0], 0)),
                pl.BlockSpec((depth, 2 * HEAD), lambda i, place: (0, i)),
                pl.BlockSpec((depth, 2 * HEAD), lambda i, place: (0, i)),
            ],
            out_specs=[
                pl.BlockSpec((2, HALF, 2 * HEAD), lambda i, place: (i, 0, 0)),
                pl.BlockSpec((2, HALF, 2 * HEAD), lambda i, place: (i, 0, 0)),
            ],
            scratch_shapes=[pltpu.VMEM((TOK, depth), BF)],
        ),
        out_shape=(out, out),
        compiler_params=params(),
        name="project",
    )(place, tokens, tokens, key_weight, value_weight)


def pack_body(keep, recv, out):
    total = keep[...] + recv[...]
    key = total[:, :, :HEAD]
    high = key.astype(BF)
    out[:, :, :HEAD] = high
    out[:, :, HEAD : 2 * HEAD] = (key - high.astype(F32)).astype(BF)
    out[:, :, 2 * HEAD :] = total[:, :, HEAD:].astype(BF)


def pack(keep, recv):
    return pl.pallas_call(
        pack_body,
        grid=(CHIPS // 2,),
        in_specs=[pl.BlockSpec((2, HALF, 2 * HEAD), lambda i: (i, 0, 0))] * 2,
        out_specs=pl.BlockSpec((2, HALF, 3 * HEAD), lambda i: (i, 0, 0)),
        out_shape=jax.ShapeDtypeStruct((CHIPS, HALF, 3 * HEAD), BF),
        compiler_params=params(),
        name="pack",
    )(keep, recv)


def own_sequences(place):
    row = lax.broadcasted_iota(jnp.int32, (HALF, HEAD), 0) + place[0] * HALF
    found = [row >= place[1 + seq] for seq in range(1, SEQS)]
    return found


def token_factor(place, scale, sequences):
    rows = [scale[pl.ds(place[5 + seq], 1), :] for seq in range(SEQS)]
    factor = jnp.broadcast_to(rows[0], (HALF, HEAD))
    for seq in range(1, SEQS):
        factor = jnp.where(sequences[seq - 1], rows[seq], factor)
    return factor


def finish_body(place, parts, key_scale, value_scale, base, low):
    total = parts[0].astype(F32)
    for chip in range(1, CHIPS):
        total = total + parts[chip].astype(F32)
    sequences = own_sequences(place)
    key = total[:, :HEAD] + total[:, HEAD : 2 * HEAD]
    value = total[:, 2 * HEAD :]
    base[:, :HEAD] = key
    base[:, HEAD:] = value
    low[:, :HEAD] = (key * token_factor(place, key_scale, sequences)).astype(BF)
    low[:, HEAD:] = (value * token_factor(place, value_scale, sequences)).astype(BF)


def finish(place, parts, key_scale, value_scale):
    scale_spec = pl.BlockSpec((NT, HEAD), lambda i, place: (0, place[9]))
    whole = pl.BlockSpec((HALF, 2 * HEAD), lambda i, place: (0, 0))
    return pl.pallas_call(
        finish_body,
        grid_spec=pltpu.PrefetchScalarGridSpec(
            num_scalar_prefetch=1,
            grid=(1,),
            in_specs=[
                pl.BlockSpec((CHIPS, HALF, 3 * HEAD), lambda i, place: (0, 0, 0)),
                scale_spec,
                scale_spec,
            ],
            out_specs=[whole, whole],
        ),
        out_shape=(
            jax.ShapeDtypeStruct((HALF, 2 * HEAD), F32),
            jax.ShapeDtypeStruct((HALF, 2 * HEAD), BF),
        ),
        compiler_params=params(),
        name="finish",
    )(place, parts, key_scale, value_scale)


def contract_last(left, right):
    return lax.dot_general(left, right, (((1,), (1,)), ((), ())), preferred_element_type=F32)


def attention_body(place, mine, other, queries, out_grad, send, keep, tile, grads):
    core = place[0]
    own_rows = pl.ds(pl.multiple_of(core * HALF, HALF), HALF)
    other_rows = pl.ds(pl.multiple_of((1 - core) * HALF, HALF), HALF)
    tile[own_rows, :] = mine[...]
    tile[other_rows, :] = other[...]
    grads[...] = jnp.zeros_like(grads)
    heads = queries.shape[1] // HEAD
    for block in range(TOK // BLOCK):
        first = max(0, block - 2) * BLOCK
        reach = (block + 1) * BLOCK - first
        rows = slice(block * BLOCK, (block + 1) * BLOCK)
        visible = slice(first, first + reach)
        key_row = lax.broadcasted_iota(jnp.int32, (reach, BLOCK), 0) + first
        query_row = lax.broadcasted_iota(jnp.int32, (reach, BLOCK), 1) + block * BLOCK
        start = jnp.zeros((reach, BLOCK), jnp.int32)
        for seq in range(1, SEQS):
            start = jnp.where(query_row >= place[1 + seq], place[1 + seq], start)
        allowed = (key_row >= start) & (key_row <= query_row)
        bias = jnp.where(allowed, 0.0, -1e30).astype(F32)
        bias = jnp.concatenate([bias, bias], axis=1)
        key_tile = tile[visible, :HEAD]
        value_tile = tile[visible, HEAD:]
        key_total = jnp.zeros((reach, HEAD), F32)
        value_total = jnp.zeros((reach, HEAD), F32)
        for pair in range(heads // 2):
            columns = [slice(h * HEAD, (h + 1) * HEAD) for h in (2 * pair, 2 * pair + 1)]
            query = jnp.concatenate([queries[rows, c] for c in columns], axis=0)
            out = jnp.concatenate([out_grad[rows, c] for c in columns], axis=0)
            scores = contract_last(key_tile, query) + bias
            peak = jnp.max(scores, axis=0, keepdims=True)
            exps = jnp.exp2((scores - peak) * (SCALE * LOG2E))
            probs = exps * (1.0 / jnp.sum(exps, axis=0, keepdims=True))
            probs_low = probs.astype(BF)
            prob_grad = contract_last(value_tile, out)
            delta = jnp.sum(probs_low.astype(F32) * prob_grad, axis=0, keepdims=True)
            score_grad = (probs * (prob_grad - delta)).astype(BF)
            value_total += jnp.dot(probs_low, out, preferred_element_type=F32)
            key_total += jnp.dot(score_grad, query, preferred_element_type=F32)
        grads[visible, :HEAD] += key_total
        grads[visible, HEAD:] += value_total
    for rows, target in ((other_rows, send), (own_rows, keep)):
        target[:, :HEAD] = grads[rows, :HEAD] * SCALE
        target[:, HEAD:] = grads[rows, HEAD:]


def attention(place, mine, other, queries, out_grad):
    out = jax.ShapeDtypeStruct((HALF, 2 * HEAD), F32)
    vmem = pl.BlockSpec(memory_space=pltpu.VMEM)
    return pl.pallas_call(
        attention_body,
        in_specs=[pl.BlockSpec(memory_space=pltpu.SMEM)] + [vmem] * 4,
        out_specs=[vmem, vmem],
        out_shape=(out, out),
        scratch_shapes=[pltpu.VMEM((TOK, 2 * HEAD), BF), pltpu.VMEM((TOK, 2 * HEAD), F32)],
        compiler_params=params(),
        name="attention",
    )(place, mine, other, queries, out_grad)


def scale_body(place, keep, recv, base, key_scale, value_scale, low, sums):
    sequences = own_sequences(place)
    for part, scale in enumerate((key_scale, value_scale)):
        columns = slice(part * HEAD, (part + 1) * HEAD)
        grad = keep[:, columns] + recv[:, columns]
        low[:, columns] = (grad * token_factor(place, scale, sequences)).astype(BF)
        product = grad * base[:, columns]
        later = [jnp.sum(product, axis=0, keepdims=True)]
        for seq in range(1, SEQS):
            later.append(jnp.sum(jnp.where(sequences[seq - 1], product, 0.0), axis=0, keepdims=True))
        later.append(jnp.zeros_like(later[0]))
        row = lax.broadcasted_iota(jnp.int32, (NT, HEAD), 0)
        table = jnp.zeros((NT, HEAD), F32)
        for seq in range(SEQS):
            table = table + jnp.where(row == place[5 + seq], later[seq] - later[seq + 1], 0.0)
        sums[:, columns] = table


def scale_grads(place, keep, recv, base, key_scale, value_scale):
    scale_spec = pl.BlockSpec((NT, HEAD), lambda i, place: (0, place[9]))
    whole = pl.BlockSpec((HALF, 2 * HEAD), lambda i, place: (0, 0))
    return pl.pallas_call(
        scale_body,
        grid_spec=pltpu.PrefetchScalarGridSpec(
            num_scalar_prefetch=1,
            grid=(1,),
            in_specs=[whole, whole, whole, scale_spec, scale_spec],
            out_specs=[whole, pl.BlockSpec((NT, 2 * HEAD), lambda i, place: (0, 0))],
        ),
        out_shape=(
            jax.ShapeDtypeStruct((HALF, 2 * HEAD), BF),
            jax.ShapeDtypeStruct((NT, 2 * HEAD), F32),
        ),
        compiler_params=params(),
        name="scale_grads",
    )(place, keep, recv, base, key_scale, value_scale)


def input_body(place, mine, other, kw, vw, out):
    core = place[0]
    for index, source in ((core, mine), (1 - core, other)):
        total = jnp.zeros((HALF, out.shape[1]), F32)
        for part, weight in enumerate((kw, vw)):
            left = jnp.concatenate(
                [source[chip, :, part * HEAD : (part + 1) * HEAD] for chip in range(CHIPS)], axis=1
            )
            total += contract_last(left, weight[...])
        out[pl.ds(pl.multiple_of(index * HALF, HALF), HALF), :] = total.astype(BF)


def input_grads(place, mine, other, key_weight, value_weight):
    features = key_weight.shape[0]
    width = features // 4
    gathered = pl.BlockSpec((CHIPS, HALF, 2 * HEAD), lambda i, place: (0, 0, 0))
    weight = pl.BlockSpec((width, CHIPS * HEAD), lambda i, place: (i, 0))
    return pl.pallas_call(
        input_body,
        grid_spec=pltpu.PrefetchScalarGridSpec(
            num_scalar_prefetch=1,
            grid=(4,),
            in_specs=[gathered, gathered, weight, weight],
            out_specs=pl.BlockSpec((TOK, width), lambda i, place: (0, i)),
        ),
        out_shape=jax.ShapeDtypeStruct((TOK, features), BF),
        compiler_params=params(),
        name="input_grads",
    )(place, mine, other, key_weight, value_weight)


def core_swap(array):
    return lax.ppermute(array, "tensor", CORE_SWAP)


def chip_exchange(array):
    return lax.all_to_all(array, "tensor", 0, 0, axis_index_groups=SAME_CORE, tiled=True)


def on_device(
    tokens,
    queries,
    out_grad,
    key_weight,
    value_weight,
    key_scale,
    value_scale,
    segment_ids,
    tenant_ids,
):
    rank = lax.axis_index("tensor")
    core, chip = rank % 2, rank // 2
    before = segment_ids[0][None, :] < jnp.arange(SEQS, dtype=jnp.int32)[:, None]
    starts = jnp.sum(before.astype(jnp.int32), axis=1)
    place = jnp.concatenate(
        [core.reshape(1), starts, tenant_ids[0], chip.reshape(1)]
    ).astype(jnp.int32)
    send, keep = project(place, tokens, key_weight, value_weight)
    packed = pack(keep, core_swap(send))
    base, low = finish(place, chip_exchange(packed), key_scale, value_scale)
    send, keep = attention(place, low, core_swap(low), queries, out_grad)
    grad_low, sums = scale_grads(place, keep, core_swap(send), base, key_scale, value_scale)
    spread = jnp.broadcast_to(grad_low[None], (CHIPS,) + grad_low.shape)
    gathered = chip_exchange(spread)
    input_grad = input_grads(place, gathered, core_swap(gathered), key_weight, value_weight)
    quarter = HEAD // 2
    halves = [lax.dynamic_slice_in_dim(sums, p * HEAD + core * quarter, quarter, 1) for p in (0, 1)]
    gives = [
        lax.dynamic_slice_in_dim(sums, p * HEAD + (1 - core) * quarter, quarter, 1) for p in (0, 1)
    ]
    own = jnp.concatenate(halves, axis=1) + core_swap(jnp.concatenate(gives, axis=1))
    for bit in range(4):
        own = own + lax.ppermute(own, "dp", [(i, i ^ 1 << bit) for i in range(16)])
    return input_grad, own[:, :quarter], own[:, quarter:]


def solution(mesh):
    return jax.shard_map(
        on_device,
        mesh=mesh,
        in_specs=(
            P("dp", "tensor"),
            P("dp", "tensor"),
            P("dp", "tensor"),
            P("tensor", None),
            P("tensor", None),
            P(),
            P(),
            P("dp", None),
            P("dp", None),
        ),
        out_specs=(P("dp", "tensor"), P(None, "tensor"), P(None, "tensor")),
        check_vma=False,
    )
```

```python
import functools

import jax
import jax.numpy as jnp
from jax import lax
from jax.experimental import pallas as pl
from jax.experimental.pallas import tpu as pltpu
from jax.sharding import PartitionSpec as P

SEQS = 4
NT = 32
HEAD = 128
TOK = 512
HALF = 256
CHIPS = 8
BLOCK = 128
LOG2E = 1.4426950408889634
SCALE = HEAD**-0.5
BF = jnp.bfloat16
F32 = jnp.float32
MIB = 1024 * 1024


def call(name, body, outs, args, scratch=(), mib=16, flops=0, out_space=pltpu.VMEM):
    spaces = [pltpu.SMEM if array.ndim == 1 else pltpu.VMEM for array in args]
    placed = [
        array if space is pltpu.SMEM else pltpu.with_memory_space_constraint(array, space)
        for array, space in zip(args, spaces)
    ]
    nbytes = sum(array.size * array.dtype.itemsize for array in args)
    return pl.pallas_call(
        body,
        in_specs=[pl.BlockSpec(memory_space=space) for space in spaces],
        out_specs=[pl.BlockSpec(memory_space=out_space)] * len(outs),
        out_shape=[out_space(*out) for out in outs],
        scratch_shapes=list(scratch),
        compiler_params=pltpu.CompilerParams(vmem_limit_bytes=mib * MIB),
        cost_estimate=pl.CostEstimate(flops=flops, bytes_accessed=nbytes, transcendentals=0),
        name=name,
    )(*placed)


def device_index(x, y, core):
    return (x % 4 * 2 + y) * 2 + core


def tensor_pairs(step):
    places = [(x, y, core) for x in range(4) for y in range(2) for core in range(2)]
    return [(device_index(*place), device_index(*step(*place))) for place in places]


CORE_SWAP = tensor_pairs(lambda x, y, core: (x, y, core ^ 1))
ROW_SWAP = tensor_pairs(lambda x, y, core: (x, y ^ 1, core))


def chip_shift(across, row):
    return tensor_pairs(lambda x, y, core: (x + across, y ^ row, core))


X_FROM = [tensor_pairs(lambda x, y, core, step=step: (x - step, y, core)) for step in range(4)]
SAME_CORE = [[chip * 2 + core for chip in range(CHIPS)] for core in range(2)]


def home_of(chip, across, row):
    home = lax.rem(chip + 2 * across, CHIPS)
    return home + row * (1 - 2 * lax.rem(home, 2))


def project_body(flip, count, tokens, *refs):
    weights, outs = refs[:count], refs[count:]
    core = lax.rem(lax.axis_index("tensor"), 2)
    half = 1 - core if flip else core
    rows = pl.ds(pl.multiple_of(half * HALF, HALF), HALF)
    for weight, out in zip(weights, outs):
        out[...] = jnp.dot(tokens[rows, :], weight[...], preferred_element_type=F32).astype(out.dtype)


def project(name, flip, tokens, weights, dtypes):
    depth, columns = weights[0].shape
    count = len(weights)
    return call(
        name,
        functools.partial(project_body, flip, count),
        [((HALF, columns), dtype) for dtype in dtypes],
        [tokens, *weights],
        flops=2 * count * HALF * depth * columns,
    )


def pack_body(key_keep, value_keep, key_recv, value_recv, out):
    for chip in range(CHIPS):
        columns = slice(chip * HEAD, (chip + 1) * HEAD)
        key = key_keep[:, columns] + key_recv[:, columns]
        high = key.astype(BF)
        out[chip, :, :HEAD] = high
        out[chip, :, HEAD : 2 * HEAD] = (key - high.astype(F32)).astype(BF)
        value = value_keep[:, columns] + value_recv[:, columns].astype(F32)
        out[chip, :, 2 * HEAD :] = value.astype(BF)


def pack(*parts):
    return call("pack", pack_body, [((CHIPS, HALF, 3 * HEAD), BF)], parts)[0]


def place_body(segments, tenants, place):
    rank = lax.axis_index("tensor")
    place[0] = lax.rem(rank, 2)
    for seq in range(SEQS):
        place[1 + seq] = jnp.sum((segments[...] < seq).astype(jnp.int32))
        place[5 + seq] = tenants[0, seq]
    place[9] = lax.div(rank, 2)


def find_place(segment_ids, tenant_ids):
    smem = pl.BlockSpec(memory_space=pltpu.SMEM)
    return pl.pallas_call(
        place_body,
        in_specs=[pl.BlockSpec(memory_space=pltpu.VMEM), smem],
        out_specs=smem,
        out_shape=jax.ShapeDtypeStruct((10,), jnp.int32),
        compiler_params=pltpu.CompilerParams(vmem_limit_bytes=4 * MIB),
        name="place",
    )(segment_ids, tenant_ids)


def own_sequences(place):
    row = lax.broadcasted_iota(jnp.int32, (HALF, HEAD), 0) + place[0] * HALF
    found = [row >= place[1 + seq] for seq in range(1, SEQS)]
    return found


def token_factor(place, scale, sequences):
    columns = pl.ds(pl.multiple_of(place[9] * HEAD, HEAD), HEAD)
    table = scale[:, columns]
    tenant = lax.broadcasted_iota(jnp.int32, table.shape, 0)
    rows = [
        jnp.sum(jnp.where(tenant == place[5 + seq], table, 0.0), axis=0, keepdims=True)
        for seq in range(SEQS)
    ]
    factor = jnp.broadcast_to(rows[0], (HALF, HEAD))
    for seq in range(1, SEQS):
        factor = jnp.where(sequences[seq - 1], rows[seq], factor)
    return factor


def finish_body(place, parts, key_scale, value_scale, base, low):
    total = parts[0].astype(F32)
    for chip in range(1, CHIPS):
        total = total + parts[chip].astype(F32)
    sequences = own_sequences(place)
    key = total[:, :HEAD] + total[:, HEAD : 2 * HEAD]
    value = total[:, 2 * HEAD :]
    base[:, :HEAD] = key
    base[:, HEAD:] = value
    low[:, :HEAD] = (key * token_factor(place, key_scale, sequences)).astype(BF)
    low[:, HEAD:] = (value * token_factor(place, value_scale, sequences)).astype(BF)


def finish(*args):
    return call("finish", finish_body, [((HALF, 2 * HEAD), F32), ((HALF, 2 * HEAD), BF)], args)


def contract_last(left, right):
    return lax.dot_general(left, right, (((1,), (1,)), ((), ())), preferred_element_type=F32)


def attention_body(place, mine, other, queries, out_grad, send, keep, tile, grads):
    core = place[0]
    own_rows = pl.ds(pl.multiple_of(core * HALF, HALF), HALF)
    other_rows = pl.ds(pl.multiple_of((1 - core) * HALF, HALF), HALF)
    tile[own_rows, :] = mine[...]
    tile[other_rows, :] = other[...]
    grads[...] = jnp.zeros_like(grads)
    heads = queries.shape[1] // HEAD
    for block in range(TOK // BLOCK):
        first = max(0, block - 2) * BLOCK
        reach = (block + 1) * BLOCK - first
        rows = slice(block * BLOCK, (block + 1) * BLOCK)
        visible = slice(first, first + reach)
        key_row = lax.broadcasted_iota(jnp.int32, (reach, BLOCK), 0) + first
        query_row = lax.broadcasted_iota(jnp.int32, (reach, BLOCK), 1) + block * BLOCK
        start = jnp.zeros((reach, BLOCK), jnp.int32)
        for seq in range(1, SEQS):
            start = jnp.where(query_row >= place[1 + seq], place[1 + seq], start)
        allowed = (key_row >= start) & (key_row <= query_row)
        bias = jnp.where(allowed, 0.0, -1e30).astype(F32)
        bias = jnp.concatenate([bias, bias], axis=1)
        key_tile = tile[visible, :HEAD]
        value_tile = tile[visible, HEAD:]
        key_total = jnp.zeros((reach, HEAD), F32)
        value_total = jnp.zeros((reach, HEAD), F32)
        for pair in range(heads // 2):
            columns = [slice(h * HEAD, (h + 1) * HEAD) for h in (2 * pair, 2 * pair + 1)]
            query = jnp.concatenate([queries[rows, c] for c in columns], axis=0)
            out = jnp.concatenate([out_grad[rows, c] for c in columns], axis=0)
            scores = contract_last(key_tile, query) + bias
            peak = jnp.max(scores, axis=0, keepdims=True)
            exps = jnp.exp2((scores - peak) * (SCALE * LOG2E))
            probs = exps * (1.0 / jnp.sum(exps, axis=0, keepdims=True))
            probs_low = probs.astype(BF)
            prob_grad = contract_last(value_tile, out)
            delta = jnp.sum(probs_low.astype(F32) * prob_grad, axis=0, keepdims=True)
            score_grad = (probs * (prob_grad - delta)).astype(BF)
            value_total += jnp.dot(probs_low, out, preferred_element_type=F32)
            key_total += jnp.dot(score_grad, query, preferred_element_type=F32)
        grads[visible, :HEAD] += key_total
        grads[visible, HEAD:] += value_total
    for rows, target in ((other_rows, send), (own_rows, keep)):
        target[:, :HEAD] = grads[rows, :HEAD] * SCALE
        target[:, HEAD:] = grads[rows, HEAD:]


def attention(*args):
    return call(
        "attention",
        attention_body,
        [((HALF, 2 * HEAD), F32)] * 2,
        args,
        scratch=[pltpu.VMEM((TOK, 2 * HEAD), BF), pltpu.VMEM((TOK, 2 * HEAD), F32)],
        mib=24,
    )


def scale_body(place, keep, recv, base, key_scale, value_scale, low, sums):
    sequences = own_sequences(place)
    tables = []
    for part, scale in enumerate((key_scale, value_scale)):
        columns = slice(part * HEAD, (part + 1) * HEAD)
        grad = keep[:, columns] + recv[:, columns]
        low[:, columns] = (grad * token_factor(place, scale, sequences)).astype(BF)
        product = grad * base[:, columns]
        later = [jnp.sum(product, axis=0, keepdims=True)]
        for seq in range(1, SEQS):
            later.append(jnp.sum(jnp.where(sequences[seq - 1], product, 0.0), axis=0, keepdims=True))
        later.append(jnp.zeros_like(later[0]))
        row = lax.broadcasted_iota(jnp.int32, (NT, HEAD), 0)
        table = jnp.zeros((NT, HEAD), F32)
        for seq in range(SEQS):
            table = table + jnp.where(row == place[5 + seq], later[seq] - later[seq + 1], 0.0)
        tables.append(table)
    key, value = tables
    lower = lax.broadcasted_iota(jnp.int32, (NT, HEAD), 1) < HEAD // 2
    first = jnp.where(lower, key, pltpu.roll(value, HEAD // 2, 1))
    second = jnp.where(lower, pltpu.roll(key, HEAD // 2, 1), value)
    sums[0] = jnp.where(place[0] == 0, first, second)
    sums[1] = jnp.where(place[0] == 0, second, first)


def scale_grads(*args):
    outs = [((HALF, 2 * HEAD), BF), ((2, NT, HEAD), F32)]
    return call("scale_grads", scale_body, outs, args)


def input_body(place, *refs):
    mine, other = refs[: CHIPS // 2], refs[CHIPS // 2 : CHIPS]
    key_weight, value_weight, out, left_key, left_value, totals, sems = refs[CHIPS:]
    core, chip = place[0], place[9]
    for half, pieces in ((core, mine), (1 - core, other)):
        rows = pl.ds(pl.multiple_of(half * HALF, HALF), HALF)
        for step, piece in enumerate(pieces):
            for row in range(2):
                columns = pl.ds(pl.multiple_of(home_of(chip, step, row) * HEAD, HEAD), HEAD)
                left_key[rows, columns] = piece[row, :, :HEAD]
                left_value[rows, columns] = piece[row, :, HEAD:]
    writes = []
    steps, width = totals.shape[0], totals.shape[2]
    for step in range(steps):
        columns = pl.ds(step * width, width)
        total = contract_last(left_key[...], key_weight[columns, :])
        total += contract_last(left_value[...], value_weight[columns, :])
        totals[step] = total.astype(BF)
        writes.append(pltpu.make_async_copy(totals.at[step], out.at[:, columns], sems.at[step]))
        writes[-1].start()
    for write in writes:
        write.wait()


def input_grads(place, mine, other, key_weight, value_weight):
    features, depth = key_weight.shape
    steps = 4
    scratch = [
        pltpu.VMEM((TOK, depth), BF),
        pltpu.VMEM((TOK, depth), BF),
        pltpu.VMEM((steps, TOK, features // steps), BF),
        pltpu.SemaphoreType.DMA((steps,)),
    ]
    outs = [((TOK, features), BF)]
    args = [place, *mine, *other, key_weight, value_weight]
    flops = 4 * TOK * features * depth
    return call("input_grads", input_body, outs, args, scratch, 20, flops, out_space=pltpu.HBM)[0]


def pair_body(mine, other, out):
    out[0] = mine[...]
    out[1] = other[...]


def pair_up(mine, other):
    return call("pair", pair_body, [((2,) + mine.shape, BF)], [mine, other])[0]


def add_body(*refs):
    total = refs[0][...]
    for ref in refs[1:-1]:
        total = total + ref[...]
    refs[-1][...] = total


def add_up(*parts):
    return call("add_up", add_body, [(parts[0].shape, F32)], parts, mib=4)[0]


def ring_body(below, here, above, three, two):
    two[...] = here[...] + above[...]
    three[...] = two[...] + below[...]


def ring_sums(*parts):
    return call("ring_sums", ring_body, [(parts[0].shape, F32)] * 2, parts, mib=4)


def split_body(first, second, third, own, give):
    total = first[...] + second[...] + third[...]
    own[...] = total[0]
    give[...] = total[1]


def split_sums(*parts):
    return call("split_sums", split_body, [((NT, HEAD), F32)] * 2, parts, mib=4)


def total_body(own, recv, key, value):
    total = own[...] + recv[...]
    key[...] = total[:, : HEAD // 2]
    value[...] = total[:, HEAD // 2 :]


def tenant_totals(own, recv):
    return pl.pallas_call(
        total_body,
        out_shape=[jax.ShapeDtypeStruct((NT, HEAD // 2), F32)] * 2,
        compiler_params=pltpu.CompilerParams(vmem_limit_bytes=4 * MIB),
        name="tenant_totals",
    )(own, recv)


def core_swap(array):
    return lax.ppermute(array, "tensor", CORE_SWAP)


def depth_from(array, step):
    pairs = [((z + step) % 8 * 2 + row, z * 2 + row) for z in range(8) for row in range(2)]
    return lax.ppermute(array, "dp", pairs)


def on_device(
    tokens,
    queries,
    out_grad,
    key_weight,
    value_weight,
    key_scale,
    value_scale,
    segment_ids,
    tenant_ids,
):
    place = find_place(segment_ids, tenant_ids)
    key_send = project("project_key", True, tokens, [key_weight], [F32])[0]
    key_recv = core_swap(key_send)
    value_send = project("project_value", True, tokens, [value_weight], [BF])[0]
    value_recv = core_swap(value_send)
    weights = [key_weight, value_weight]
    key_keep, value_keep = project("project_keep", False, tokens, weights, [F32, F32])
    packed = pack(key_keep, value_keep, key_recv, value_recv)
    packed, place = lax.optimization_barrier((packed, place))
    parts = lax.all_to_all(packed, "tensor", 0, 0, axis_index_groups=SAME_CORE, tiled=True)
    base, low = finish(place, parts, key_scale, value_scale)
    send, keep = attention(place, low, core_swap(low), queries, out_grad)
    grad_low, sums = scale_grads(place, keep, core_swap(send), base, key_scale, value_scale)
    sums = add_up(sums, lax.ppermute(sums, "dp", [(i, i ^ 1) for i in range(16)]))
    pair = pair_up(grad_low, lax.ppermute(grad_low, "tensor", ROW_SWAP))
    pair, sums = lax.optimization_barrier((pair, sums))
    near = [lax.ppermute(pair, "tensor", X_FROM[step]) for step in (2, 1, 3)]
    three, two = ring_sums(depth_from(sums, -1), sums, depth_from(sums, 1))
    own, give = split_sums(three, depth_from(three, 3), depth_from(two, -3))
    near, own, give = lax.optimization_barrier((near, own, give))
    mine = [pair, near[1], near[0], near[2]]
    other = [core_swap(piece) for piece in mine]
    input_grad = input_grads(place, mine, other, key_weight, value_weight)
    key_total, value_total = tenant_totals(own, core_swap(give))
    return input_grad, key_total, value_total


def solution(mesh):
    return jax.shard_map(
        on_device,
        mesh=mesh,
        in_specs=(
            P("dp", "tensor"),
            P("dp", "tensor"),
            P("dp", "tensor"),
            P("tensor", None),
            P("tensor", None),
            P(),
            P(),
            P("dp", None),
            P("dp", None),
        ),
        out_specs=(P("dp", "tensor"), P(None, "tensor"), P(None, "tensor")),
        check_vma=False,
    )
```

```python
import functools

import jax
import jax.numpy as jnp
from jax import lax
from jax.experimental import pallas as pl
from jax.experimental.pallas import tpu as pltpu
from jax.sharding import PartitionSpec as P

SEQS = 4
NT = 32
HEAD = 128
TOK = 512
HALF = 256
CHIPS = 8
BLOCK = 128
LOG2E = 1.4426950408889634
SCALE = HEAD**-0.5
BF = jnp.bfloat16
F32 = jnp.float32
MIB = 1024 * 1024


def call(name, body, outs, args, scratch=(), mib=16, flops=0, out_space=pltpu.VMEM):
    spaces = [pltpu.SMEM if array.ndim == 1 else pltpu.VMEM for array in args]
    placed = [
        array if space is pltpu.SMEM else pltpu.with_memory_space_constraint(array, space)
        for array, space in zip(args, spaces)
    ]
    nbytes = sum(array.size * array.dtype.itemsize for array in args)
    return pl.pallas_call(
        body,
        in_specs=[pl.BlockSpec(memory_space=space) for space in spaces],
        out_specs=[pl.BlockSpec(memory_space=out_space)] * len(outs),
        out_shape=[out_space(*out) for out in outs],
        scratch_shapes=list(scratch),
        compiler_params=pltpu.CompilerParams(vmem_limit_bytes=mib * MIB),
        cost_estimate=pl.CostEstimate(flops=flops, bytes_accessed=nbytes, transcendentals=0),
        name=name,
    )(*placed)


def device_index(x, y, core):
    return (x % 4 * 2 + y) * 2 + core


def tensor_pairs(step):
    places = [(x, y, core) for x in range(4) for y in range(2) for core in range(2)]
    return [(device_index(*place), device_index(*step(*place))) for place in places]


CORE_SWAP = tensor_pairs(lambda x, y, core: (x, y, core ^ 1))
X_ORDER = [0, 2, 1, 3]
SENT = [(2, 1), (1, 1), (3, 1), (1, 0), (3, 0)]
KEPT = [(2, 0), (0, 1), (0, 0)]


def home_of(chip, across, row):
    home = lax.rem(chip + 2 * across, CHIPS)
    return home + row * (1 - 2 * lax.rem(home, 2))


def project_body(flip, count, tokens, *refs):
    weights, outs = refs[:count], refs[count:]
    core = lax.rem(lax.axis_index("tensor"), 2)
    half = 1 - core if flip else core
    rows = pl.ds(pl.multiple_of(half * HALF, HALF), HALF)
    for weight, out in zip(weights, outs):
        out[...] = jnp.dot(tokens[rows, :], weight[...], preferred_element_type=F32).astype(out.dtype)


def project(name, flip, tokens, weights, dtypes):
    depth, columns = weights[0].shape
    count = len(weights)
    return call(
        name,
        functools.partial(project_body, flip, count),
        [((HALF, columns), dtype) for dtype in dtypes],
        [tokens, *weights],
        flops=2 * count * HALF * depth * columns,
    )


def encode(total, out):
    high = total[:, :HEAD].astype(BF)
    out[:, :HEAD] = high
    out[:, HEAD : 2 * HEAD] = (total[:, :HEAD] - high.astype(F32)).astype(BF)
    out[:, 2 * HEAD :] = total[:, HEAD:].astype(BF)


def decode(part):
    key = part[:, :HEAD].astype(F32) + part[:, HEAD : 2 * HEAD].astype(F32)
    return jnp.concatenate([key, part[:, 2 * HEAD :].astype(F32)], axis=1)


def pack_body(key_keep, value_keep, key_recv, value_recv, *outs):
    chip = lax.div(lax.axis_index("tensor"), 2)
    for (across, row), out in zip(SENT + KEPT, outs):
        columns = pl.ds(pl.multiple_of(home_of(chip, across, row) * HEAD, HEAD), HEAD)
        key = key_keep[:, columns] + key_recv[:, columns]
        value = value_keep[:, columns] + value_recv[:, columns].astype(F32)
        total = jnp.concatenate([key, value], axis=1)
        if (across, row) in KEPT:
            out[...] = total
        else:
            encode(total, out)


def pack(*parts):
    outs = [((HALF, 3 * HEAD), BF)] * len(SENT) + [((HALF, 2 * HEAD), F32)] * len(KEPT)
    return call("pack", pack_body, outs, parts)


def relay_body(kept, *refs):
    total = kept[...]
    for part in refs[:-1]:
        total = total + decode(part[...])
    encode(total, refs[-1])


def relay(*parts):
    return call("relay", relay_body, [((HALF, 3 * HEAD), BF)], parts, mib=8)[0]


def place_body(segments, tenants, place):
    rank = lax.axis_index("tensor")
    place[0] = lax.rem(rank, 2)
    for seq in range(SEQS):
        place[1 + seq] = jnp.sum((segments[...] < seq).astype(jnp.int32))
        place[5 + seq] = tenants[0, seq]
    place[9] = lax.div(rank, 2)


def find_place(segment_ids, tenant_ids):
    smem = pl.BlockSpec(memory_space=pltpu.SMEM)
    return pl.pallas_call(
        place_body,
        in_specs=[pl.BlockSpec(memory_space=pltpu.VMEM), smem],
        out_specs=smem,
        out_shape=jax.ShapeDtypeStruct((10,), jnp.int32),
        compiler_params=pltpu.CompilerParams(vmem_limit_bytes=4 * MIB),
        name="place",
    )(segment_ids, tenant_ids)


def own_sequences(place):
    row = lax.broadcasted_iota(jnp.int32, (HALF, HEAD), 0) + place[0] * HALF
    found = [row >= place[1 + seq] for seq in range(1, SEQS)]
    return found


def token_factor(place, scale, sequences):
    columns = pl.ds(pl.multiple_of(place[9] * HEAD, HEAD), HEAD)
    table = scale[:, columns]
    tenant = lax.broadcasted_iota(jnp.int32, table.shape, 0)
    rows = [
        jnp.sum(jnp.where(tenant == place[5 + seq], table, 0.0), axis=0, keepdims=True)
        for seq in range(SEQS)
    ]
    factor = jnp.broadcast_to(rows[0], (HALF, HEAD))
    for seq in range(1, SEQS):
        factor = jnp.where(sequences[seq - 1], rows[seq], factor)
    return factor


def finish_body(place, kept, *refs):
    parts, (key_scale, value_scale, base, low) = refs[:-4], refs[-4:]
    total = kept[...]
    for part in parts:
        total = total + decode(part[...])
    sequences = own_sequences(place)
    key = total[:, :HEAD]
    value = total[:, HEAD:]
    base[:, :HEAD] = key
    base[:, HEAD:] = value
    low[:, :HEAD] = (key * token_factor(place, key_scale, sequences)).astype(BF)
    low[:, HEAD:] = (value * token_factor(place, value_scale, sequences)).astype(BF)


def finish(*args):
    return call("finish", finish_body, [((HALF, 2 * HEAD), F32), ((HALF, 2 * HEAD), BF)], args)


def contract_last(left, right):
    return lax.dot_general(left, right, (((1,), (1,)), ((), ())), preferred_element_type=F32)


def attention_body(place, mine, other, queries, out_grad, send, keep, tile, grads):
    core = place[0]
    own_rows = pl.ds(pl.multiple_of(core * HALF, HALF), HALF)
    other_rows = pl.ds(pl.multiple_of((1 - core) * HALF, HALF), HALF)
    tile[own_rows, :] = mine[...]
    tile[other_rows, :] = other[...]
    grads[...] = jnp.zeros_like(grads)
    heads = queries.shape[1] // HEAD
    for block in range(TOK // BLOCK):
        first = max(0, block - 2) * BLOCK
        reach = (block + 1) * BLOCK - first
        rows = slice(block * BLOCK, (block + 1) * BLOCK)
        visible = slice(first, first + reach)
        key_row = lax.broadcasted_iota(jnp.int32, (reach, BLOCK), 0) + first
        query_row = lax.broadcasted_iota(jnp.int32, (reach, BLOCK), 1) + block * BLOCK
        start = jnp.zeros((reach, BLOCK), jnp.int32)
        for seq in range(1, SEQS):
            start = jnp.where(query_row >= place[1 + seq], place[1 + seq], start)
        allowed = (key_row >= start) & (key_row <= query_row)
        bias = jnp.where(allowed, 0.0, -1e30).astype(F32)
        bias = jnp.concatenate([bias, bias], axis=1)
        key_tile = tile[visible, :HEAD]
        value_tile = tile[visible, HEAD:]
        key_total = jnp.zeros((reach, HEAD), F32)
        value_total = jnp.zeros((reach, HEAD), F32)
        for pair in range(heads // 2):
            columns = [slice(h * HEAD, (h + 1) * HEAD) for h in (2 * pair, 2 * pair + 1)]
            query = jnp.concatenate([queries[rows, c] for c in columns], axis=0)
            out = jnp.concatenate([out_grad[rows, c] for c in columns], axis=0)
            scores = contract_last(key_tile, query) + bias
            peak = jnp.max(scores, axis=0, keepdims=True)
            exps = jnp.exp2((scores - peak) * (SCALE * LOG2E))
            probs = exps * (1.0 / jnp.sum(exps, axis=0, keepdims=True))
            probs_low = probs.astype(BF)
            prob_grad = contract_last(value_tile, out)
            delta = jnp.sum(probs_low.astype(F32) * prob_grad, axis=0, keepdims=True)
            score_grad = (probs * (prob_grad - delta)).astype(BF)
            value_total += jnp.dot(probs_low, out, preferred_element_type=F32)
            key_total += jnp.dot(score_grad, query, preferred_element_type=F32)
        grads[visible, :HEAD] += key_total
        grads[visible, HEAD:] += value_total
    for rows, target in ((other_rows, send), (own_rows, keep)):
        target[:, :HEAD] = grads[rows, :HEAD] * SCALE
        target[:, HEAD:] = grads[rows, HEAD:]


def attention(*args):
    return call(
        "attention",
        attention_body,
        [((HALF, 2 * HEAD), F32)] * 2,
        args,
        scratch=[pltpu.VMEM((TOK, 2 * HEAD), BF), pltpu.VMEM((TOK, 2 * HEAD), F32)],
        mib=24,
    )


def scale_body(place, keep, recv, base, key_scale, value_scale, low, own, give):
    sequences = own_sequences(place)
    tables = []
    for part, scale in enumerate((key_scale, value_scale)):
        columns = slice(part * HEAD, (part + 1) * HEAD)
        grad = keep[:, columns] + recv[:, columns]
        low[:, columns] = (grad * token_factor(place, scale, sequences)).astype(BF)
        product = grad * base[:, columns]
        later = [jnp.sum(product, axis=0, keepdims=True)]
        for seq in range(1, SEQS):
            later.append(jnp.sum(jnp.where(sequences[seq - 1], product, 0.0), axis=0, keepdims=True))
        later.append(jnp.zeros_like(later[0]))
        row = lax.broadcasted_iota(jnp.int32, (NT, HEAD), 0)
        table = jnp.zeros((NT, HEAD), F32)
        for seq in range(SEQS):
            table = table + jnp.where(row == place[5 + seq], later[seq] - later[seq + 1], 0.0)
        tables.append(table)
    key, value = tables
    lower = lax.broadcasted_iota(jnp.int32, (NT, HEAD), 1) < HEAD // 2
    first = jnp.where(lower, key, pltpu.roll(value, HEAD // 2, 1))
    second = jnp.where(lower, pltpu.roll(key, HEAD // 2, 1), value)
    own[...] = jnp.where(place[0] == 0, first, second)
    give[...] = jnp.where(place[0] == 0, second, first)


def scale_grads(*args):
    outs = [((HALF, 2 * HEAD), BF), ((NT, HEAD), F32), ((NT, HEAD), F32)]
    return call("scale_grads", scale_body, outs, args)


def input_body(place, *refs):
    mine, other = refs[: CHIPS // 2], refs[CHIPS // 2 : CHIPS]
    key_weight, value_weight, out, left_key, left_value, totals, sems = refs[CHIPS:]
    core, chip = place[0], place[9]
    for half, pieces in ((core, mine), (1 - core, other)):
        rows = pl.ds(pl.multiple_of(half * HALF, HALF), HALF)
        for across, piece in zip(X_ORDER, pieces):
            for row in range(2):
                columns = pl.ds(pl.multiple_of(home_of(chip, across, row) * HEAD, HEAD), HEAD)
                left_key[rows, columns] = piece[row, :, :HEAD]
                left_value[rows, columns] = piece[row, :, HEAD:]
    writes = []
    steps, width = totals.shape[0], totals.shape[2]
    for step in range(steps):
        columns = pl.ds(step * width, width)
        total = contract_last(left_key[...], key_weight[columns, :])
        total += contract_last(left_value[...], value_weight[columns, :])
        totals[step] = total.astype(BF)
        writes.append(pltpu.make_async_copy(totals.at[step], out.at[:, columns], sems.at[step]))
        writes[-1].start()
    for write in writes:
        write.wait()


def input_grads(place, mine, other, key_weight, value_weight):
    features, depth = key_weight.shape
    steps = 4
    scratch = [
        pltpu.VMEM((TOK, depth), BF),
        pltpu.VMEM((TOK, depth), BF),
        pltpu.VMEM((steps, TOK, features // steps), BF),
        pltpu.SemaphoreType.DMA((steps,)),
    ]
    outs = [((TOK, features), BF)]
    args = [place, *mine, *other, key_weight, value_weight]
    flops = 4 * TOK * features * depth
    return call("input_grads", input_body, outs, args, scratch, 20, flops, out_space=pltpu.HBM)[0]


def add_body(*refs):
    total = refs[0][...]
    for ref in refs[1:-1]:
        total = total + ref[...]
    refs[-1][...] = total


def add_up(*parts):
    return call("add_up", add_body, [(parts[0].shape, F32)], parts, mib=4)[0]


def pair_body(mine, other, here, below, above, out, three, two):
    out[0] = mine[...]
    out[1] = other[...]
    two[...] = here[...] + above[...]
    three[...] = two[...] + below[...]


def pair_up(*args):
    outs = [((2,) + args[0].shape, BF), (args[2].shape, F32), (args[2].shape, F32)]
    return call("pair", pair_body, outs, args, mib=4)


def total_body(here, recv, key, value):
    total = here[...] + recv[...]
    key[...] = total[:, : HEAD // 2]
    value[...] = total[:, HEAD // 2 :]


def tenant_totals(here, recv):
    return pl.pallas_call(
        total_body,
        out_shape=[jax.ShapeDtypeStruct((NT, HEAD // 2), F32)] * 2,
        compiler_params=pltpu.CompilerParams(vmem_limit_bytes=4 * MIB),
        name="tenant_totals",
    )(here, recv)


def core_swap(array):
    return lax.ppermute(array, "tensor", CORE_SWAP)


def chip_from(array, across, row):
    if across == row == 0:
        return array
    pairs = tensor_pairs(lambda x, y, core: (x - across, y ^ row, core))
    return lax.ppermute(array, "tensor", pairs)


def depth_from(array, step):
    pairs = [((z + step) % 8 * 2 + row, z * 2 + row) for z in range(8) for row in range(2)]
    return lax.ppermute(array, "dp", pairs)


def on_device(
    tokens,
    queries,
    out_grad,
    key_weight,
    value_weight,
    key_scale,
    value_scale,
    segment_ids,
    tenant_ids,
):
    place = find_place(segment_ids, tenant_ids)
    key_send = project("project_key", True, tokens, [key_weight], [F32])[0]
    key_recv = core_swap(key_send)
    value_send = project("project_value", True, tokens, [value_weight], [BF])[0]
    value_recv = core_swap(value_send)
    weights = [key_weight, value_weight]
    key_keep, value_keep = project("project_keep", False, tokens, weights, [F32, F32])
    packed = pack(key_keep, value_keep, key_recv, value_recv)
    part_21, part_11, part_31, part_10, part_30, kept_20, kept_01, kept_00 = packed
    part_20 = relay(kept_20, chip_from(part_21, 0, 1))
    part_01 = relay(kept_01, chip_from(part_11, -1, 0), chip_from(part_31, 1, 0))
    parts = [
        chip_from(part_10, -1, 0),
        chip_from(part_30, 1, 0),
        chip_from(part_20, 2, 0),
        chip_from(part_01, 0, 1),
    ]
    base, low = finish(place, kept_00, *parts, key_scale, value_scale)
    send, keep = attention(place, low, core_swap(low), queries, out_grad)
    grad_low, own, give = scale_grads(place, keep, core_swap(send), base, key_scale, value_scale)
    sums = add_up(own, core_swap(give))
    arrived = lax.optimization_barrier(
        (chip_from(grad_low, 0, 1), sums, depth_from(sums, -1), depth_from(sums, 1))
    )
    pair, three, two = pair_up(grad_low, *arrived)
    near = [chip_from(pair, across, 0) for across in X_ORDER[1:]]
    far = [depth_from(three, 3), depth_from(two, -3)]
    near, far = lax.optimization_barrier((near, far))
    sums = add_up(three, *far)
    sums_other = lax.ppermute(sums, "dp", [(i, i ^ 1) for i in range(16)])
    mine = [pair] + near
    other = [core_swap(piece) for piece in mine]
    input_grad = input_grads(place, mine, other, key_weight, value_weight)
    input_grad, sums_other = lax.optimization_barrier((input_grad, sums_other))
    key_total, value_total = tenant_totals(sums, sums_other)
    return input_grad, key_total, value_total


def solution(mesh):
    return jax.shard_map(
        on_device,
        mesh=mesh,
        in_specs=(
            P("dp", "tensor"),
            P("dp", "tensor"),
            P("dp", "tensor"),
            P("tensor", None),
            P("tensor", None),
            P(),
            P(),
            P("dp", None),
            P("dp", None),
        ),
        out_specs=(P("dp", "tensor"), P(None, "tensor"), P(None, "tensor")),
        check_vma=False,
    )
```

```python
import functools

import jax
import jax.numpy as jnp
from jax import lax
from jax.experimental import pallas as pl
from jax.experimental.pallas import tpu as pltpu
from jax.sharding import PartitionSpec as P

SEQS = 4
NT = 32
HEAD = 128
TOK = 512
HALF = 256
CHIPS = 8
BLOCK = 128
LOG2E = 1.4426950408889634
SCALE = HEAD**-0.5
BF = jnp.bfloat16
F32 = jnp.float32
MIB = 1024 * 1024


def call(name, body, outs, args, scratch=(), mib=16, flops=0, out_space=pltpu.VMEM):
    spaces = [pltpu.SMEM if array.ndim == 1 else pltpu.VMEM for array in args]
    placed = [
        array if space is pltpu.SMEM else pltpu.with_memory_space_constraint(array, space)
        for array, space in zip(args, spaces)
    ]
    nbytes = sum(array.size * array.dtype.itemsize for array in args)
    return pl.pallas_call(
        body,
        in_specs=[pl.BlockSpec(memory_space=space) for space in spaces],
        out_specs=[pl.BlockSpec(memory_space=out_space)] * len(outs),
        out_shape=[out_space(*out) for out in outs],
        scratch_shapes=list(scratch),
        compiler_params=pltpu.CompilerParams(vmem_limit_bytes=mib * MIB),
        cost_estimate=pl.CostEstimate(flops=flops, bytes_accessed=nbytes, transcendentals=0),
        name=name,
    )(*placed)


def device_index(x, y, core):
    return (x % 4 * 2 + y) * 2 + core


def tensor_pairs(step):
    places = [(x, y, core) for x in range(4) for y in range(2) for core in range(2)]
    return [(device_index(*place), device_index(*step(*place))) for place in places]


CORE_SWAP = tensor_pairs(lambda x, y, core: (x, y, core ^ 1))
ORDER = [(0, 0), (0, 1), (2, 0), (1, 0), (1, 1), (3, 0), (3, 1), (2, 1)]
SENT = [(2, 1), (1, 1), (3, 1), (1, 0), (3, 0)]
KEPT = [(2, 0), (0, 1), (0, 0)]


def home_of(chip, across, row):
    home = lax.rem(chip + 2 * across, CHIPS)
    return home + row * (1 - 2 * lax.rem(home, 2))


def project_body(flip, count, tokens, *refs):
    weights, outs = refs[:count], refs[count:]
    core = lax.rem(lax.axis_index("tensor"), 2)
    half = 1 - core if flip else core
    rows = pl.ds(pl.multiple_of(half * HALF, HALF), HALF)
    for weight, out in zip(weights, outs):
        out[...] = jnp.dot(tokens[rows, :], weight[...], preferred_element_type=F32).astype(out.dtype)


def project(name, flip, tokens, weights, dtypes):
    depth, columns = weights[0].shape
    count = len(weights)
    return call(
        name,
        functools.partial(project_body, flip, count),
        [((HALF, columns), dtype) for dtype in dtypes],
        [tokens, *weights],
        flops=2 * count * HALF * depth * columns,
    )


def encode(total, out):
    high = total[:, :HEAD].astype(BF)
    out[:, :HEAD] = high
    out[:, HEAD : 2 * HEAD] = (total[:, :HEAD] - high.astype(F32)).astype(BF)
    out[:, 2 * HEAD :] = total[:, HEAD:].astype(BF)


def decode(part):
    key = part[:, :HEAD].astype(F32) + part[:, HEAD : 2 * HEAD].astype(F32)
    return jnp.concatenate([key, part[:, 2 * HEAD :].astype(F32)], axis=1)


def pack_body(key_keep, value_keep, key_recv, value_recv, *outs):
    chip = lax.div(lax.axis_index("tensor"), 2)
    for (across, row), out in zip(SENT + KEPT, outs):
        columns = pl.ds(pl.multiple_of(home_of(chip, across, row) * HEAD, HEAD), HEAD)
        key = key_keep[:, columns] + key_recv[:, columns]
        value = value_keep[:, columns] + value_recv[:, columns].astype(F32)
        total = jnp.concatenate([key, value], axis=1)
        if (across, row) in KEPT:
            out[...] = total
        else:
            encode(total, out)


def pack(*parts):
    outs = [((HALF, 3 * HEAD), BF)] * len(SENT) + [((HALF, 2 * HEAD), F32)] * len(KEPT)
    return call("pack", pack_body, outs, parts)


def relay_body(kept, *refs):
    total = kept[...]
    for part in refs[:-1]:
        total = total + decode(part[...])
    encode(total, refs[-1])


def relay(*parts):
    return call("relay", relay_body, [((HALF, 3 * HEAD), BF)], parts, mib=8)[0]


def place_body(segments, tenants, place):
    rank = lax.axis_index("tensor")
    place[0] = lax.rem(rank, 2)
    for seq in range(SEQS):
        place[1 + seq] = jnp.sum((segments[...] < seq).astype(jnp.int32))
        place[5 + seq] = tenants[0, seq]
    place[9] = lax.div(rank, 2)


def find_place(segment_ids, tenant_ids):
    smem = pl.BlockSpec(memory_space=pltpu.SMEM)
    return pl.pallas_call(
        place_body,
        in_specs=[pl.BlockSpec(memory_space=pltpu.VMEM), smem],
        out_specs=smem,
        out_shape=jax.ShapeDtypeStruct((10,), jnp.int32),
        compiler_params=pltpu.CompilerParams(vmem_limit_bytes=4 * MIB),
        name="place",
    )(segment_ids, tenant_ids)


def own_sequences(place):
    row = lax.broadcasted_iota(jnp.int32, (HALF, HEAD), 0) + place[0] * HALF
    found = [row >= place[1 + seq] for seq in range(1, SEQS)]
    return found


def token_factor(place, scale, sequences):
    columns = pl.ds(pl.multiple_of(place[9] * HEAD, HEAD), HEAD)
    table = scale[:, columns]
    tenant = lax.broadcasted_iota(jnp.int32, table.shape, 0)
    rows = [
        jnp.sum(jnp.where(tenant == place[5 + seq], table, 0.0), axis=0, keepdims=True)
        for seq in range(SEQS)
    ]
    factor = jnp.broadcast_to(rows[0], (HALF, HEAD))
    for seq in range(1, SEQS):
        factor = jnp.where(sequences[seq - 1], rows[seq], factor)
    return factor


def finish_body(place, kept, *refs):
    parts, (key_scale, value_scale, base, low) = refs[:-4], refs[-4:]
    total = kept[...]
    for part in parts:
        total = total + decode(part[...])
    sequences = own_sequences(place)
    key = total[:, :HEAD]
    value = total[:, HEAD:]
    base[:, :HEAD] = key
    base[:, HEAD:] = value
    low[:, :HEAD] = (key * token_factor(place, key_scale, sequences)).astype(BF)
    low[:, HEAD:] = (value * token_factor(place, value_scale, sequences)).astype(BF)


def finish(*args):
    return call("finish", finish_body, [((HALF, 2 * HEAD), F32), ((HALF, 2 * HEAD), BF)], args)


def contract_last(left, right):
    return lax.dot_general(left, right, (((1,), (1,)), ((), ())), preferred_element_type=F32)


def attention_body(place, mine, other, queries, out_grad, send, keep, tile, grads):
    core = place[0]
    own_rows = pl.ds(pl.multiple_of(core * HALF, HALF), HALF)
    other_rows = pl.ds(pl.multiple_of((1 - core) * HALF, HALF), HALF)
    tile[own_rows, :] = mine[...]
    tile[other_rows, :] = other[...]
    grads[...] = jnp.zeros_like(grads)
    heads = queries.shape[1] // HEAD
    for block in range(TOK // BLOCK):
        first = max(0, block - 2) * BLOCK
        reach = (block + 1) * BLOCK - first
        rows = slice(block * BLOCK, (block + 1) * BLOCK)
        visible = slice(first, first + reach)
        key_row = lax.broadcasted_iota(jnp.int32, (reach, BLOCK), 0) + first
        query_row = lax.broadcasted_iota(jnp.int32, (reach, BLOCK), 1) + block * BLOCK
        start = jnp.zeros((reach, BLOCK), jnp.int32)
        for seq in range(1, SEQS):
            start = jnp.where(query_row >= place[1 + seq], place[1 + seq], start)
        allowed = (key_row >= start) & (key_row <= query_row)
        bias = jnp.where(allowed, 0.0, -1e30).astype(F32)
        bias = jnp.concatenate([bias, bias], axis=1)
        key_tile = tile[visible, :HEAD]
        value_tile = tile[visible, HEAD:]
        key_total = jnp.zeros((reach, HEAD), F32)
        value_total = jnp.zeros((reach, HEAD), F32)
        for pair in range(heads // 2):
            columns = [slice(h * HEAD, (h + 1) * HEAD) for h in (2 * pair, 2 * pair + 1)]
            query = jnp.concatenate([queries[rows, c] for c in columns], axis=0)
            out = jnp.concatenate([out_grad[rows, c] for c in columns], axis=0)
            scores = contract_last(key_tile, query) + bias
            peak = jnp.max(scores, axis=0, keepdims=True)
            exps = jnp.exp2((scores - peak) * (SCALE * LOG2E))
            probs = exps * (1.0 / jnp.sum(exps, axis=0, keepdims=True))
            probs_low = probs.astype(BF)
            prob_grad = contract_last(value_tile, out)
            delta = jnp.sum(probs_low.astype(F32) * prob_grad, axis=0, keepdims=True)
            score_grad = (probs * (prob_grad - delta)).astype(BF)
            value_total += jnp.dot(probs_low, out, preferred_element_type=F32)
            key_total += jnp.dot(score_grad, query, preferred_element_type=F32)
        grads[visible, :HEAD] += key_total
        grads[visible, HEAD:] += value_total
    for rows, target in ((other_rows, send), (own_rows, keep)):
        target[:, :HEAD] = grads[rows, :HEAD] * SCALE
        target[:, HEAD:] = grads[rows, HEAD:]


def attention(*args):
    return call(
        "attention",
        attention_body,
        [((HALF, 2 * HEAD), F32)] * 2,
        args,
        scratch=[pltpu.VMEM((TOK, 2 * HEAD), BF), pltpu.VMEM((TOK, 2 * HEAD), F32)],
        mib=24,
    )


def scale_body(place, keep, recv, key_scale, value_scale, low):
    sequences = own_sequences(place)
    for part, scale in enumerate((key_scale, value_scale)):
        columns = slice(part * HEAD, (part + 1) * HEAD)
        grad = keep[:, columns] + recv[:, columns]
        low[:, columns] = (grad * token_factor(place, scale, sequences)).astype(BF)


def scale_grads(*args):
    return call("scale_grads", scale_body, [((HALF, 2 * HEAD), BF)], args)[0]


def table_body(place, keep, send, base, base_other, sums):
    width = 2 * HEAD
    totals = [jnp.zeros((1, width), F32)] * (SEQS + 1)
    for half, grad, values in ((place[0], keep, base), (1 - place[0], send, base_other)):
        product = grad[...] * values[...]
        row = lax.broadcasted_iota(jnp.int32, product.shape, 0) + half * HALF
        totals[0] += jnp.sum(product, axis=0, keepdims=True)
        for seq in range(1, SEQS):
            later = jnp.where(row >= place[1 + seq], product, 0.0)
            totals[seq] += jnp.sum(later, axis=0, keepdims=True)
    tenant = lax.broadcasted_iota(jnp.int32, sums.shape, 0)
    table = jnp.zeros(sums.shape, F32)
    for seq in range(SEQS):
        table += jnp.where(tenant == place[5 + seq], totals[seq] - totals[seq + 1], 0.0)
    sums[...] = table


def tenant_table(*args):
    return call("tenant_table", table_body, [((NT, 2 * HEAD), F32)], args, mib=8)[0]


def order_body(key_weight, value_weight, out):
    chip = lax.div(lax.axis_index("tensor"), 2)
    for index, (across, row) in enumerate(ORDER):
        columns = pl.ds(pl.multiple_of(home_of(chip, across, row) * HEAD, HEAD), HEAD)
        start = 2 * index * HEAD
        out[:, start : start + HEAD] = key_weight[:, columns]
        out[:, start + HEAD : start + 2 * HEAD] = value_weight[:, columns]


def order_weights(key_weight, value_weight):
    features, depth = key_weight.shape
    outs = [((features, 2 * depth), BF)]
    return call("order_weights", order_body, outs, [key_weight, value_weight])[0]


def place_rows(place, left, mine, other):
    for half, pieces in ((place[0], mine), (1 - place[0], other)):
        rows = pl.ds(pl.multiple_of(half * HALF, HALF), HALF)
        chunks = [piece[row] for piece in pieces for row in range(piece.shape[0])]
        for index, chunk in enumerate(chunks):
            left[rows, 2 * index * HEAD : 2 * (index + 1) * HEAD] = chunk


def near_body(place, mine, mine_far, other, other_far, weight, out, left):
    place_rows(place, left, [mine, mine_far], [other, other_far])
    out[...] = contract_last(left[...], weight[:, : left.shape[1]])


def near_grads(place, mine, other, weight):
    features = weight.shape[0]
    scratch = [pltpu.VMEM((TOK, 6 * HEAD), BF)]
    outs = [((TOK, features), F32)]
    flops = 2 * TOK * features * 6 * HEAD
    args = [place, *mine, *other, weight]
    return call("near_grads", near_body, outs, args, scratch, 8, flops)[0]


def far_body(place, *refs):
    count = len(refs) // 2 - 3
    mine, other = refs[:count], refs[count : 2 * count]
    near, weight, out, left, totals, sems = refs[2 * count :]
    place_rows(place, left, mine, other)
    writes = []
    steps, width = totals.shape[0], totals.shape[2]
    for step in range(steps):
        columns = pl.ds(step * width, width)
        total = contract_last(left[...], weight[columns, weight.shape[1] - left.shape[1] :])
        totals[step] = (near[:, columns] + total).astype(BF)
        writes.append(pltpu.make_async_copy(totals.at[step], out.at[:, columns], sems.at[step]))
        writes[-1].start()
    for write in writes:
        write.wait()


def far_grads(place, mine, other, near, weight):
    features = weight.shape[0]
    depth = 10 * HEAD
    steps = 4
    scratch = [
        pltpu.VMEM((TOK, depth), BF),
        pltpu.VMEM((steps, TOK, features // steps), BF),
        pltpu.SemaphoreType.DMA((steps,)),
    ]
    outs = [((TOK, features), BF)]
    args = [place, *mine, *other, near, weight]
    flops = 2 * TOK * features * depth
    return call("far_grads", far_body, outs, args, scratch, 16, flops, out_space=pltpu.HBM)[0]


def add_body(*refs):
    total = refs[0][...]
    for ref in refs[1:-1]:
        total = total + ref[...]
    refs[-1][...] = total


def add_up(*parts):
    return call("add_up", add_body, [(parts[0].shape, F32)], parts, mib=4)[0]


def pair_body(mine, other, out):
    out[0] = mine[...]
    out[1] = other[...]


def pair_up(mine, other):
    return call("pair", pair_body, [((2,) + mine.shape, BF)], [mine, other], mib=4)[0]


def own_core():
    return lax.rem(lax.axis_index("tensor"), 2)


def ring_body(here, direct, swapped, three, give):
    total = here[...] + direct[...]
    full = total + swapped[...]
    three[...] = full
    give[...] = jnp.where(own_core() == 0, full, total)


def ring_sums(*parts):
    return call("ring_sums", ring_body, [(parts[0].shape, F32)] * 2, parts, mib=4)


def ring_end_body(three, recv, out):
    out[...] = jnp.where(own_core() == 0, three[...], 0.0) + recv[...]


def ring_end(*parts):
    return call("ring_end", ring_end_body, [(parts[0].shape, F32)], parts, mib=4)[0]


def total_body(here, recv, key, value):
    total = here[...] + recv[...]
    own = lax.broadcasted_iota(jnp.int32, (NT, HEAD // 2), 1) >= 0
    own = own & (own_core() == 0)
    key[...] = jnp.where(own, total[:, : HEAD // 2], total[:, HEAD // 2 : HEAD])
    value[...] = jnp.where(own, total[:, HEAD : HEAD + HEAD // 2], total[:, HEAD + HEAD // 2 :])


def tenant_totals(here, recv):
    return pl.pallas_call(
        total_body,
        out_shape=[jax.ShapeDtypeStruct((NT, HEAD // 2), F32)] * 2,
        compiler_params=pltpu.CompilerParams(vmem_limit_bytes=4 * MIB),
        name="tenant_totals",
    )(here, recv)


def core_swap(array):
    return lax.ppermute(array, "tensor", CORE_SWAP)


def chip_from(array, across, row):
    if across == row == 0:
        return array
    pairs = tensor_pairs(lambda x, y, core: (x - across, y ^ row, core))
    return lax.ppermute(array, "tensor", pairs)


def depth_from(array, steps):
    pairs = []
    for z in range(8):
        for row in range(2):
            for chip in range(CHIPS):
                for core in range(2):
                    source = (z + steps[core]) % 8 * 2 + row
                    place = chip * 2 + core
                    pairs.append((source * 16 + place, (z * 2 + row) * 16 + place))
    return lax.ppermute(array, ("dp", "tensor"), pairs)


def on_device(
    tokens,
    queries,
    out_grad,
    key_weight,
    value_weight,
    key_scale,
    value_scale,
    segment_ids,
    tenant_ids,
):
    place = find_place(segment_ids, tenant_ids)
    key_send = project("project_key", True, tokens, [key_weight], [F32])[0]
    key_recv = core_swap(key_send)
    value_send = project("project_value", True, tokens, [value_weight], [BF])[0]
    value_recv = core_swap(value_send)
    weights = [key_weight, value_weight]
    key_keep, value_keep = project("project_keep", False, tokens, weights, [F32, F32])
    packed = pack(key_keep, value_keep, key_recv, value_recv)
    part_21, part_11, part_31, part_10, part_30, kept_20, kept_01, kept_00 = packed
    part_20 = relay(kept_20, chip_from(part_21, 0, 1))
    part_01 = relay(kept_01, chip_from(part_11, -1, 0), chip_from(part_31, 1, 0))
    parts = [
        chip_from(part_10, -1, 0),
        chip_from(part_30, 1, 0),
        chip_from(part_20, 2, 0),
        chip_from(part_01, 0, 1),
    ]
    weight = order_weights(key_weight, value_weight)
    parts, weight, place = lax.optimization_barrier((parts, weight, place))
    base, low = finish(place, kept_00, *parts, key_scale, value_scale)
    low_other = core_swap(low)
    base_other = core_swap(base)
    send, keep = attention(place, low, low_other, queries, out_grad)
    recv = core_swap(send)
    sums = tenant_table(place, keep, send, base, base_other)
    recv, sums = lax.optimization_barrier((recv, sums))
    grad_low = scale_grads(place, keep, recv, key_scale, value_scale)
    grad_low, sums_other = lax.optimization_barrier((grad_low, core_swap(sums)))
    sums = add_up(sums, sums_other)
    row_part, far_part, ring = lax.optimization_barrier(
        (chip_from(grad_low, 0, 1), chip_from(grad_low, 2, 0), depth_from(sums, (-1, 1)))
    )
    pair = pair_up(grad_low, row_part)
    three, give = ring_sums(sums, ring, core_swap(ring))
    early = [pair, far_part[None]]
    near = near_grads(place, early, [core_swap(piece) for piece in early], weight)
    arrived = [chip_from(pair, 1, 0), chip_from(pair, 3, 0), chip_from(far_part, 0, 1)]
    arrived, ring, near = lax.optimization_barrier((arrived, depth_from(give, (3, -3)), near))
    arrived = arrived[:2] + [arrived[2][None]]
    sums = ring_end(three, ring)
    others, sums_other = lax.optimization_barrier(
        ([core_swap(piece) for piece in arrived], core_swap(sums))
    )
    sums = add_up(sums, sums_other)
    row_sums = lax.ppermute(sums, "dp", [(i, i ^ 1) for i in range(16)])
    input_grad = far_grads(place, arrived, others, near, weight)
    input_grad, row_sums = lax.optimization_barrier((input_grad, row_sums))
    key_total, value_total = tenant_totals(sums, row_sums)
    return input_grad, key_total, value_total


def solution(mesh):
    return jax.shard_map(
        on_device,
        mesh=mesh,
        in_specs=(
            P("dp", "tensor"),
            P("dp", "tensor"),
            P("dp", "tensor"),
            P("tensor", None),
            P("tensor", None),
            P(),
            P(),
            P("dp", None),
            P("dp", None),
        ),
        out_specs=(P("dp", "tensor"), P(None, "tensor"), P(None, "tensor")),
        check_vma=False,
    )
```

```python
import functools

import jax
import jax.numpy as jnp
from jax import lax
from jax.experimental import pallas as pl
from jax.experimental.pallas import tpu as pltpu
from jax.sharding import PartitionSpec as P

SEQS = 4
NT = 32
HEAD = 128
TOK = 512
HALF = 256
CHIPS = 8
BLOCK = 128
LOG2E = 1.4426950408889634
SCALE = HEAD**-0.5
BF = jnp.bfloat16
F32 = jnp.float32
MIB = 1024 * 1024


def call(name, body, outs, args, scratch=(), mib=16, flops=0, out_space=pltpu.VMEM):
    spaces = [pltpu.SMEM if array.ndim == 1 else pltpu.VMEM for array in args]
    placed = [
        array if space is pltpu.SMEM else pltpu.with_memory_space_constraint(array, space)
        for array, space in zip(args, spaces)
    ]
    nbytes = sum(array.size * array.dtype.itemsize for array in args)
    return pl.pallas_call(
        body,
        in_specs=[pl.BlockSpec(memory_space=space) for space in spaces],
        out_specs=[pl.BlockSpec(memory_space=out_space)] * len(outs),
        out_shape=[out_space(*out) for out in outs],
        scratch_shapes=list(scratch),
        compiler_params=pltpu.CompilerParams(vmem_limit_bytes=mib * MIB),
        cost_estimate=pl.CostEstimate(flops=flops, bytes_accessed=nbytes, transcendentals=0),
        name=name,
    )(*placed)


def device_index(x, y, core):
    return (x % 4 * 2 + y) * 2 + core


def tensor_pairs(step):
    places = [(x, y, core) for x in range(4) for y in range(2) for core in range(2)]
    return [(device_index(*place), device_index(*step(*place))) for place in places]


CORE_SWAP = tensor_pairs(lambda x, y, core: (x, y, core ^ 1))
ORDER = [(0, 0), (0, 1), (2, 0), (1, 0), (1, 1), (3, 0), (3, 1), (2, 1)]
SENT = [(2, 1), (1, 1), (3, 1), (1, 0), (3, 0)]
KEPT = [(2, 0), (0, 1), (0, 0)]


def home_of(chip, across, row):
    home = lax.rem(chip + 2 * across, CHIPS)
    return home + row * (1 - 2 * lax.rem(home, 2))


def project_body(flip, count, tokens, *refs):
    weights, outs = refs[:count], refs[count:]
    core = lax.rem(lax.axis_index("tensor"), 2)
    half = 1 - core if flip else core
    rows = pl.ds(pl.multiple_of(half * HALF, HALF), HALF)
    for weight, out in zip(weights, outs):
        out[...] = jnp.dot(tokens[rows, :], weight[...], preferred_element_type=F32).astype(out.dtype)


def project(name, flip, tokens, weights, dtypes):
    depth, columns = weights[0].shape
    count = len(weights)
    return call(
        name,
        functools.partial(project_body, flip, count),
        [((HALF, columns), dtype) for dtype in dtypes],
        [tokens, *weights],
        flops=2 * count * HALF * depth * columns,
    )


def encode(total, out):
    high = total[:, :HEAD].astype(BF)
    out[:, :HEAD] = high
    out[:, HEAD : 2 * HEAD] = (total[:, :HEAD] - high.astype(F32)).astype(BF)
    out[:, 2 * HEAD :] = total[:, HEAD:].astype(BF)


def decode(part):
    key = part[:, :HEAD].astype(F32) + part[:, HEAD : 2 * HEAD].astype(F32)
    return jnp.concatenate([key, part[:, 2 * HEAD :].astype(F32)], axis=1)


def pack_body(key_keep, value_keep, key_recv, value_recv, *outs):
    chip = lax.div(lax.axis_index("tensor"), 2)
    for (across, row), out in zip(SENT + KEPT, outs):
        columns = pl.ds(pl.multiple_of(home_of(chip, across, row) * HEAD, HEAD), HEAD)
        key = key_keep[:, columns] + key_recv[:, columns]
        value = value_keep[:, columns] + value_recv[:, columns].astype(F32)
        total = jnp.concatenate([key, value], axis=1)
        if (across, row) in KEPT:
            out[...] = total
        else:
            encode(total, out)


def pack(*parts):
    outs = [((HALF, 3 * HEAD), BF)] * len(SENT) + [((HALF, 2 * HEAD), F32)] * len(KEPT)
    return call("pack", pack_body, outs, parts)


def relay_body(kept, *refs):
    total = kept[...]
    for part in refs[:-1]:
        total = total + decode(part[...])
    encode(total, refs[-1])


def relay(*parts):
    return call("relay", relay_body, [((HALF, 3 * HEAD), BF)], parts, mib=8)[0]


def place_body(segments, tenants, place):
    rank = lax.axis_index("tensor")
    place[0] = lax.rem(rank, 2)
    for seq in range(SEQS):
        place[1 + seq] = jnp.sum((segments[...] < seq).astype(jnp.int32))
        place[5 + seq] = tenants[0, seq]
    place[9] = lax.div(rank, 2)


def find_place(segment_ids, tenant_ids):
    smem = pl.BlockSpec(memory_space=pltpu.SMEM)
    return pl.pallas_call(
        place_body,
        in_specs=[pl.BlockSpec(memory_space=pltpu.VMEM), smem],
        out_specs=smem,
        out_shape=jax.ShapeDtypeStruct((10,), jnp.int32),
        compiler_params=pltpu.CompilerParams(vmem_limit_bytes=4 * MIB),
        name="place",
    )(segment_ids, tenant_ids)


def own_sequences(place):
    row = lax.broadcasted_iota(jnp.int32, (HALF, HEAD), 0) + place[0] * HALF
    found = [row >= place[1 + seq] for seq in range(1, SEQS)]
    return found


def token_factor(place, scale, sequences):
    columns = pl.ds(pl.multiple_of(place[9] * HEAD, HEAD), HEAD)
    table = scale[:, columns]
    tenant = lax.broadcasted_iota(jnp.int32, table.shape, 0)
    rows = [
        jnp.sum(jnp.where(tenant == place[5 + seq], table, 0.0), axis=0, keepdims=True)
        for seq in range(SEQS)
    ]
    factor = jnp.broadcast_to(rows[0], (HALF, HEAD))
    for seq in range(1, SEQS):
        factor = jnp.where(sequences[seq - 1], rows[seq], factor)
    return factor


def finish_body(place, kept, *refs):
    parts, (key_scale, value_scale, base, low) = refs[:-4], refs[-4:]
    total = kept[...]
    for part in parts:
        total = total + decode(part[...])
    sequences = own_sequences(place)
    key = total[:, :HEAD]
    value = total[:, HEAD:]
    base[:, :HEAD] = key
    base[:, HEAD:] = value
    low[:, :HEAD] = (key * token_factor(place, key_scale, sequences)).astype(BF)
    low[:, HEAD:] = (value * token_factor(place, value_scale, sequences)).astype(BF)


def finish(*args):
    return call("finish", finish_body, [((HALF, 2 * HEAD), F32), ((HALF, 2 * HEAD), BF)], args)


def contract_last(left, right):
    return lax.dot_general(left, right, (((1,), (1,)), ((), ())), preferred_element_type=F32)


def attention_body(place, mine, other, queries, out_grad, send, keep, tile, grads):
    core = place[0]
    own_rows = pl.ds(pl.multiple_of(core * HALF, HALF), HALF)
    other_rows = pl.ds(pl.multiple_of((1 - core) * HALF, HALF), HALF)
    tile[own_rows, :] = mine[...]
    tile[other_rows, :] = other[...]
    grads[...] = jnp.zeros_like(grads)
    heads = queries.shape[1] // HEAD
    for block in range(TOK // BLOCK):
        first = max(0, block - 2) * BLOCK
        reach = (block + 1) * BLOCK - first
        rows = slice(block * BLOCK, (block + 1) * BLOCK)
        visible = slice(first, first + reach)
        key_row = lax.broadcasted_iota(jnp.int32, (reach, BLOCK), 0) + first
        query_row = lax.broadcasted_iota(jnp.int32, (reach, BLOCK), 1) + block * BLOCK
        start = jnp.zeros((reach, BLOCK), jnp.int32)
        for seq in range(1, SEQS):
            start = jnp.where(query_row >= place[1 + seq], place[1 + seq], start)
        allowed = (key_row >= start) & (key_row <= query_row)
        bias = jnp.where(allowed, 0.0, -1e30).astype(F32)
        bias = jnp.concatenate([bias, bias], axis=1)
        key_tile = tile[visible, :HEAD]
        value_tile = tile[visible, HEAD:]
        probs_parts, score_parts, query_parts, out_parts = [], [], [], []
        for pair in range(heads // 2):
            columns = [slice(h * HEAD, (h + 1) * HEAD) for h in (2 * pair, 2 * pair + 1)]
            query = jnp.concatenate([queries[rows, c] for c in columns], axis=0)
            out = jnp.concatenate([out_grad[rows, c] for c in columns], axis=0)
            scores = contract_last(key_tile, query) + bias
            peak = jnp.max(scores, axis=0, keepdims=True)
            exps = jnp.exp2((scores - peak) * (SCALE * LOG2E))
            probs = exps * (1.0 / jnp.sum(exps, axis=0, keepdims=True))
            probs_low = probs.astype(BF)
            prob_grad = contract_last(value_tile, out)
            delta = jnp.sum(probs_low.astype(F32) * prob_grad, axis=0, keepdims=True)
            score_parts.append((probs * (prob_grad - delta)).astype(BF))
            probs_parts.append(probs_low)
            query_parts.append(query)
            out_parts.append(out)
        for part, left, right in (
            (slice(0, HEAD), score_parts, query_parts),
            (slice(HEAD, 2 * HEAD), probs_parts, out_parts),
        ):
            left, right = jnp.concatenate(left, axis=1), jnp.concatenate(right, axis=0)
            grads[visible, part] += jnp.dot(left, right, preferred_element_type=F32)
    for rows, target in ((other_rows, send), (own_rows, keep)):
        target[:, :HEAD] = grads[rows, :HEAD] * SCALE
        target[:, HEAD:] = grads[rows, HEAD:]


def attention(*args):
    return call(
        "attention",
        attention_body,
        [((HALF, 2 * HEAD), F32)] * 2,
        args,
        scratch=[pltpu.VMEM((TOK, 2 * HEAD), BF), pltpu.VMEM((TOK, 2 * HEAD), F32)],
        mib=24,
    )


def scale_body(place, keep, recv, key_scale, value_scale, low):
    sequences = own_sequences(place)
    for part, scale in enumerate((key_scale, value_scale)):
        columns = slice(part * HEAD, (part + 1) * HEAD)
        grad = keep[:, columns] + recv[:, columns]
        low[:, columns] = (grad * token_factor(place, scale, sequences)).astype(BF)


def scale_grads(*args):
    return call("scale_grads", scale_body, [((HALF, 2 * HEAD), BF)], args)[0]


def table_body(place, keep, send, base, base_other, sums):
    width = 2 * HEAD
    totals = [jnp.zeros((1, width), F32)] * (SEQS + 1)
    for half, grad, values in ((place[0], keep, base), (1 - place[0], send, base_other)):
        product = grad[...] * values[...]
        row = lax.broadcasted_iota(jnp.int32, product.shape, 0) + half * HALF
        totals[0] += jnp.sum(product, axis=0, keepdims=True)
        for seq in range(1, SEQS):
            later = jnp.where(row >= place[1 + seq], product, 0.0)
            totals[seq] += jnp.sum(later, axis=0, keepdims=True)
    tenant = lax.broadcasted_iota(jnp.int32, sums.shape, 0)
    table = jnp.zeros(sums.shape, F32)
    for seq in range(SEQS):
        table += jnp.where(tenant == place[5 + seq], totals[seq] - totals[seq + 1], 0.0)
    sums[...] = table


def tenant_table(*args):
    return call("tenant_table", table_body, [((NT, 2 * HEAD), F32)], args, mib=8)[0]


def order_body(key_weight, value_weight, out):
    chip = lax.div(lax.axis_index("tensor"), 2)
    for index, (across, row) in enumerate(ORDER):
        columns = pl.ds(pl.multiple_of(home_of(chip, across, row) * HEAD, HEAD), HEAD)
        start = 2 * index * HEAD
        out[:, start : start + HEAD] = key_weight[:, columns]
        out[:, start + HEAD : start + 2 * HEAD] = value_weight[:, columns]


def order_weights(key_weight, value_weight):
    features, depth = key_weight.shape
    outs = [((features, 2 * depth), BF)]
    return call("order_weights", order_body, outs, [key_weight, value_weight])[0]


def place_rows(place, left, mine, other):
    for half, pieces in ((place[0], mine), (1 - place[0], other)):
        rows = pl.ds(pl.multiple_of(half * HALF, HALF), HALF)
        chunks = [piece[row] for piece in pieces for row in range(piece.shape[0])]
        for index, chunk in enumerate(chunks):
            left[rows, 2 * index * HEAD : 2 * (index + 1) * HEAD] = chunk


def near_body(place, mine, mine_far, other, other_far, weight, out, left):
    place_rows(place, left, [mine, mine_far], [other, other_far])
    out[...] = contract_last(left[...], weight[:, : left.shape[1]])


def near_grads(place, mine, other, weight):
    features = weight.shape[0]
    scratch = [pltpu.VMEM((TOK, 6 * HEAD), BF)]
    outs = [((TOK, features), F32)]
    flops = 2 * TOK * features * 6 * HEAD
    args = [place, *mine, *other, weight]
    return call("near_grads", near_body, outs, args, scratch, 8, flops)[0]


def far_body(place, *refs):
    count = len(refs) // 2 - 3
    mine, other = refs[:count], refs[count : 2 * count]
    near, weight, out, left, totals, sems = refs[2 * count :]
    place_rows(place, left, mine, other)
    writes = []
    steps, width = totals.shape[0], totals.shape[2]
    for step in range(steps):
        columns = pl.ds(step * width, width)
        total = contract_last(left[...], weight[columns, weight.shape[1] - left.shape[1] :])
        totals[step] = (near[:, columns] + total).astype(BF)
        writes.append(pltpu.make_async_copy(totals.at[step], out.at[:, columns], sems.at[step]))
        writes[-1].start()
    for write in writes:
        write.wait()


def far_grads(place, mine, other, near, weight):
    features = weight.shape[0]
    depth = 10 * HEAD
    steps = 4
    scratch = [
        pltpu.VMEM((TOK, depth), BF),
        pltpu.VMEM((steps, TOK, features // steps), BF),
        pltpu.SemaphoreType.DMA((steps,)),
    ]
    outs = [((TOK, features), BF)]
    args = [place, *mine, *other, near, weight]
    flops = 2 * TOK * features * depth
    return call("far_grads", far_body, outs, args, scratch, 16, flops, out_space=pltpu.HBM)[0]


def add_body(*refs):
    total = refs[0][...]
    for ref in refs[1:-1]:
        total = total + ref[...]
    refs[-1][...] = total


def add_up(*parts):
    return call("add_up", add_body, [(parts[0].shape, F32)], parts, mib=4)[0]


def pair_body(mine, other, out):
    out[0] = mine[...]
    out[1] = other[...]


def pair_up(mine, other):
    return call("pair", pair_body, [((2,) + mine.shape, BF)], [mine, other], mib=4)[0]


def own_core():
    return lax.rem(lax.axis_index("tensor"), 2)


def ring_body(here, direct, swapped, three, give):
    total = here[...] + direct[...]
    full = total + swapped[...]
    three[...] = full
    give[...] = jnp.where(own_core() == 0, full, total)


def ring_sums(*parts):
    return call("ring_sums", ring_body, [(parts[0].shape, F32)] * 2, parts, mib=4)


def ring_end_body(three, recv, out):
    out[...] = jnp.where(own_core() == 0, three[...], 0.0) + recv[...]


def ring_end(*parts):
    return call("ring_end", ring_end_body, [(parts[0].shape, F32)], parts, mib=4)[0]


def total_body(here, recv, key, value):
    total = here[...] + recv[...]
    own = lax.broadcasted_iota(jnp.int32, (NT, HEAD // 2), 1) >= 0
    own = own & (own_core() == 0)
    key[...] = jnp.where(own, total[:, : HEAD // 2], total[:, HEAD // 2 : HEAD])
    value[...] = jnp.where(own, total[:, HEAD : HEAD + HEAD // 2], total[:, HEAD + HEAD // 2 :])


def tenant_totals(here, recv):
    return pl.pallas_call(
        total_body,
        out_shape=[jax.ShapeDtypeStruct((NT, HEAD // 2), F32)] * 2,
        compiler_params=pltpu.CompilerParams(vmem_limit_bytes=4 * MIB),
        name="tenant_totals",
    )(here, recv)


def core_swap(array):
    return lax.ppermute(array, "tensor", CORE_SWAP)


def chip_from(array, across, row):
    if across == row == 0:
        return array
    pairs = tensor_pairs(lambda x, y, core: (x - across, y ^ row, core))
    return lax.ppermute(array, "tensor", pairs)


def depth_from(array, steps):
    pairs = []
    for z in range(8):
        for row in range(2):
            for chip in range(CHIPS):
                for core in range(2):
                    source = (z + steps[core]) % 8 * 2 + row
                    place = chip * 2 + core
                    pairs.append((source * 16 + place, (z * 2 + row) * 16 + place))
    return lax.ppermute(array, ("dp", "tensor"), pairs)


def on_device(
    tokens,
    queries,
    out_grad,
    key_weight,
    value_weight,
    key_scale,
    value_scale,
    segment_ids,
    tenant_ids,
):
    place = find_place(segment_ids, tenant_ids)
    key_send = project("project_key", True, tokens, [key_weight], [F32])[0]
    key_recv = core_swap(key_send)
    value_send = project("project_value", True, tokens, [value_weight], [BF])[0]
    value_recv = core_swap(value_send)
    weights = [key_weight, value_weight]
    key_keep, value_keep = project("project_keep", False, tokens, weights, [F32, F32])
    packed = pack(key_keep, value_keep, key_recv, value_recv)
    part_21, part_11, part_31, part_10, part_30, kept_20, kept_01, kept_00 = packed
    part_20 = relay(kept_20, chip_from(part_21, 0, 1))
    part_01 = relay(kept_01, chip_from(part_11, -1, 0), chip_from(part_31, 1, 0))
    parts = [
        chip_from(part_10, -1, 0),
        chip_from(part_30, 1, 0),
        chip_from(part_20, 2, 0),
        chip_from(part_01, 0, 1),
    ]
    weight = order_weights(key_weight, value_weight)
    parts, weight, place = lax.optimization_barrier((parts, weight, place))
    base, low = finish(place, kept_00, *parts, key_scale, value_scale)
    low_other = core_swap(low)
    base_other = core_swap(base)
    send, keep = attention(place, low, low_other, queries, out_grad)
    recv = core_swap(send)
    sums = tenant_table(place, keep, send, base, base_other)
    recv, sums = lax.optimization_barrier((recv, sums))
    grad_low = scale_grads(place, keep, recv, key_scale, value_scale)
    grad_low, sums_other = lax.optimization_barrier((grad_low, core_swap(sums)))
    sums = add_up(sums, sums_other)
    row_part, far_part, ring = lax.optimization_barrier(
        (chip_from(grad_low, 0, 1), chip_from(grad_low, 2, 0), depth_from(sums, (-1, 1)))
    )
    pair = pair_up(grad_low, row_part)
    three, give = ring_sums(sums, ring, core_swap(ring))
    early = [pair, far_part[None]]
    near = near_grads(place, early, [core_swap(piece) for piece in early], weight)
    arrived = [chip_from(pair, 1, 0), chip_from(pair, 3, 0), chip_from(far_part, 0, 1)]
    arrived, ring, near = lax.optimization_barrier((arrived, depth_from(give, (3, -3)), near))
    arrived = arrived[:2] + [arrived[2][None]]
    sums = ring_end(three, ring)
    others, sums_other = lax.optimization_barrier(
        ([core_swap(piece) for piece in arrived], core_swap(sums))
    )
    sums = add_up(sums, sums_other)
    row_sums = lax.ppermute(sums, "dp", [(i, i ^ 1) for i in range(16)])
    input_grad = far_grads(place, arrived, others, near, weight)
    input_grad, row_sums = lax.optimization_barrier((input_grad, row_sums))
    key_total, value_total = tenant_totals(sums, row_sums)
    return input_grad, key_total, value_total


def solution(mesh):
    return jax.shard_map(
        on_device,
        mesh=mesh,
        in_specs=(
            P("dp", "tensor"),
            P("dp", "tensor"),
            P("dp", "tensor"),
            P("tensor", None),
            P("tensor", None),
            P(),
            P(),
            P("dp", None),
            P("dp", None),
        ),
        out_specs=(P("dp", "tensor"), P(None, "tensor"), P(None, "tensor")),
        check_vma=False,
    )
```

```python
import functools

import jax
import jax.numpy as jnp
from jax import lax
from jax.experimental import pallas as pl
from jax.experimental.pallas import tpu as pltpu
from jax.sharding import PartitionSpec as P

SEQS = 4
NT = 32
HEAD = 128
TOK = 512
HALF = 256
CHIPS = 8
BLOCK = 128
LOG2E = 1.4426950408889634
SCALE = HEAD**-0.5
BF = jnp.bfloat16
F32 = jnp.float32
MIB = 1024 * 1024


def call(name, body, outs, args, scratch=(), mib=16, flops=0, out_space=pltpu.VMEM):
    spaces = [pltpu.SMEM if array.ndim == 1 else pltpu.VMEM for array in args]
    placed = [
        array if space is pltpu.SMEM else pltpu.with_memory_space_constraint(array, space)
        for array, space in zip(args, spaces)
    ]
    nbytes = sum(array.size * array.dtype.itemsize for array in args)
    return pl.pallas_call(
        body,
        in_specs=[pl.BlockSpec(memory_space=space) for space in spaces],
        out_specs=[pl.BlockSpec(memory_space=out_space)] * len(outs),
        out_shape=[out_space(*out) for out in outs],
        scratch_shapes=list(scratch),
        compiler_params=pltpu.CompilerParams(vmem_limit_bytes=mib * MIB),
        cost_estimate=pl.CostEstimate(flops=flops, bytes_accessed=nbytes, transcendentals=0),
        name=name,
    )(*placed)


def device_index(x, y, core):
    return (x % 4 * 2 + y) * 2 + core


def tensor_pairs(step):
    places = [(x, y, core) for x in range(4) for y in range(2) for core in range(2)]
    return [(device_index(*place), device_index(*step(*place))) for place in places]


CORE_SWAP = tensor_pairs(lambda x, y, core: (x, y, core ^ 1))
ORDER = [(0, 0), (0, 1), (2, 0), (1, 0), (1, 1), (3, 0), (3, 1), (2, 1)]
SENT = [(2, 1), (1, 1), (3, 1), (1, 0), (3, 0)]
KEPT = [(2, 0), (0, 1), (0, 0)]


def load_body(tokens, key_weight, value_weight, send, rows, key_out, value_out, sems):
    core = lax.rem(lax.axis_index("tensor"), 2)
    halves = [pl.ds(pl.multiple_of(half * HALF, HALF), HALF) for half in (1 - core, core)]
    steps = 4
    width = send.shape[1] // steps
    chunks = [pl.ds(step * width, width) for step in range(steps)]
    pairs = [(tokens.at[halves[0], :], rows.at[halves[0], :])]
    pairs += [(key_weight.at[:, chunk], key_out.at[:, chunk]) for chunk in chunks]
    pairs += [(tokens.at[halves[1], :], rows.at[halves[1], :]), (value_weight, value_out)]
    copies = [pltpu.make_async_copy(*pair, sems.at[i]) for i, pair in enumerate(pairs)]
    for copy in copies:
        copy.start()
    copies[0].wait()
    for chunk, copy in zip(chunks, copies[1:]):
        copy.wait()
        send[:, chunk] = jnp.dot(
            rows[halves[0], :], key_out[:, chunk], preferred_element_type=F32
        )
    for copy in copies[steps + 1 :]:
        copy.wait()


def load_project(tokens, key_weight, value_weight):
    args = [pltpu.with_memory_space_constraint(x, pltpu.HBM) for x in (tokens, key_weight, value_weight)]
    outs = [((HALF, CHIPS * HEAD), F32)] + [(x.shape, BF) for x in args]
    return pl.pallas_call(
        load_body,
        in_specs=[pl.BlockSpec(memory_space=pltpu.HBM)] * 3,
        out_specs=[pl.BlockSpec(memory_space=pltpu.VMEM)] * 4,
        out_shape=[pltpu.VMEM(*out) for out in outs],
        scratch_shapes=[pltpu.SemaphoreType.DMA((7,))],
        compiler_params=pltpu.CompilerParams(vmem_limit_bytes=16 * MIB),
        name="project_key",
    )(*args)


def home_of(chip, across, row):
    home = lax.rem(chip + 2 * across, CHIPS)
    return home + row * (1 - 2 * lax.rem(home, 2))


def project_body(flip, count, tokens, *refs):
    weights, outs = refs[:count], refs[count:]
    core = lax.rem(lax.axis_index("tensor"), 2)
    half = 1 - core if flip else core
    rows = pl.ds(pl.multiple_of(half * HALF, HALF), HALF)
    for weight, out in zip(weights, outs):
        out[...] = jnp.dot(tokens[rows, :], weight[...], preferred_element_type=F32).astype(out.dtype)


def project(name, flip, tokens, weights, dtypes):
    depth, columns = weights[0].shape
    count = len(weights)
    return call(
        name,
        functools.partial(project_body, flip, count),
        [((HALF, columns), dtype) for dtype in dtypes],
        [tokens, *weights],
        flops=2 * count * HALF * depth * columns,
    )


def encode(total, out):
    high = total[:, :HEAD].astype(BF)
    out[:, :HEAD] = high
    out[:, HEAD : 2 * HEAD] = (total[:, :HEAD] - high.astype(F32)).astype(BF)
    out[:, 2 * HEAD :] = total[:, HEAD:].astype(BF)


def decode(part):
    key = part[:, :HEAD].astype(F32) + part[:, HEAD : 2 * HEAD].astype(F32)
    return jnp.concatenate([key, part[:, 2 * HEAD :].astype(F32)], axis=1)


def pack_body(key_keep, value_keep, key_recv, value_recv, *outs):
    chip = lax.div(lax.axis_index("tensor"), 2)
    for (across, row), out in zip(SENT + KEPT, outs):
        columns = pl.ds(pl.multiple_of(home_of(chip, across, row) * HEAD, HEAD), HEAD)
        key = key_keep[:, columns] + key_recv[:, columns]
        value = value_keep[:, columns] + value_recv[:, columns].astype(F32)
        total = jnp.concatenate([key, value], axis=1)
        if (across, row) in KEPT:
            out[...] = total
        else:
            encode(total, out)


def pack(*parts):
    outs = [((HALF, 3 * HEAD), BF)] * len(SENT) + [((HALF, 2 * HEAD), F32)] * len(KEPT)
    return call("pack", pack_body, outs, parts)


def relay_body(kept, *refs):
    total = kept[...]
    for part in refs[:-1]:
        total = total + decode(part[...])
    encode(total, refs[-1])


def relay(*parts):
    return call("relay", relay_body, [((HALF, 3 * HEAD), BF)], parts, mib=8)[0]


def place_body(segments, tenants, place):
    rank = lax.axis_index("tensor")
    place[0] = lax.rem(rank, 2)
    for seq in range(SEQS):
        place[1 + seq] = jnp.sum((segments[...] < seq).astype(jnp.int32))
        place[5 + seq] = tenants[0, seq]
    place[9] = lax.div(rank, 2)


def find_place(segment_ids, tenant_ids):
    smem = pl.BlockSpec(memory_space=pltpu.SMEM)
    return pl.pallas_call(
        place_body,
        in_specs=[pl.BlockSpec(memory_space=pltpu.VMEM), smem],
        out_specs=smem,
        out_shape=jax.ShapeDtypeStruct((10,), jnp.int32),
        compiler_params=pltpu.CompilerParams(vmem_limit_bytes=4 * MIB),
        name="place",
    )(segment_ids, tenant_ids)


def own_sequences(place):
    row = lax.broadcasted_iota(jnp.int32, (HALF, HEAD), 0) + place[0] * HALF
    found = [row >= place[1 + seq] for seq in range(1, SEQS)]
    return found


def token_factor(place, scale, sequences):
    columns = pl.ds(pl.multiple_of(place[9] * HEAD, HEAD), HEAD)
    table = scale[:, columns]
    tenant = lax.broadcasted_iota(jnp.int32, table.shape, 0)
    rows = [
        jnp.sum(jnp.where(tenant == place[5 + seq], table, 0.0), axis=0, keepdims=True)
        for seq in range(SEQS)
    ]
    factor = jnp.broadcast_to(rows[0], (HALF, HEAD))
    for seq in range(1, SEQS):
        factor = jnp.where(sequences[seq - 1], rows[seq], factor)
    return factor


def finish_body(place, kept, *refs):
    parts, (key_scale, value_scale, base, low) = refs[:-4], refs[-4:]
    total = kept[...]
    for part in parts:
        total = total + decode(part[...])
    sequences = own_sequences(place)
    key = total[:, :HEAD]
    value = total[:, HEAD:]
    base[:, :HEAD] = key
    base[:, HEAD:] = value
    low[:, :HEAD] = (key * token_factor(place, key_scale, sequences)).astype(BF)
    low[:, HEAD:] = (value * token_factor(place, value_scale, sequences)).astype(BF)


def finish(*args):
    return call("finish", finish_body, [((HALF, 2 * HEAD), F32), ((HALF, 2 * HEAD), BF)], args)


def contract_last(left, right):
    return lax.dot_general(left, right, (((1,), (1,)), ((), ())), preferred_element_type=F32)


def attention_body(place, mine, other, queries, out_grad, send, keep, tile, grads):
    core = place[0]
    own_rows = pl.ds(pl.multiple_of(core * HALF, HALF), HALF)
    other_rows = pl.ds(pl.multiple_of((1 - core) * HALF, HALF), HALF)
    tile[own_rows, :] = mine[...]
    tile[other_rows, :] = other[...]
    grads[...] = jnp.zeros_like(grads)
    heads = queries.shape[1] // HEAD
    for block in range(TOK // BLOCK):
        first = max(0, block - 2) * BLOCK
        reach = (block + 1) * BLOCK - first
        rows = slice(block * BLOCK, (block + 1) * BLOCK)
        visible = slice(first, first + reach)
        key_row = lax.broadcasted_iota(jnp.int32, (reach, BLOCK), 0) + first
        query_row = lax.broadcasted_iota(jnp.int32, (reach, BLOCK), 1) + block * BLOCK
        start = jnp.zeros((reach, BLOCK), jnp.int32)
        for seq in range(1, SEQS):
            start = jnp.where(query_row >= place[1 + seq], place[1 + seq], start)
        allowed = (key_row >= start) & (key_row <= query_row)
        bias = jnp.where(allowed, 0.0, -1e30).astype(F32)
        bias = jnp.concatenate([bias, bias], axis=1)
        key_tile = tile[visible, :HEAD]
        value_tile = tile[visible, HEAD:]
        probs_parts, score_parts, query_parts, out_parts = [], [], [], []
        for pair in range(heads // 2):
            columns = [slice(h * HEAD, (h + 1) * HEAD) for h in (2 * pair, 2 * pair + 1)]
            query = jnp.concatenate([queries[rows, c] for c in columns], axis=0)
            out = jnp.concatenate([out_grad[rows, c] for c in columns], axis=0)
            scores = contract_last(key_tile, query) + bias
            peak = jnp.max(scores, axis=0, keepdims=True)
            exps = jnp.exp2((scores - peak) * (SCALE * LOG2E))
            probs = exps * (1.0 / jnp.sum(exps, axis=0, keepdims=True))
            probs_low = probs.astype(BF)
            prob_grad = contract_last(value_tile, out)
            delta = jnp.sum(probs_low.astype(F32) * prob_grad, axis=0, keepdims=True)
            score_parts.append((probs * (prob_grad - delta)).astype(BF))
            probs_parts.append(probs_low)
            query_parts.append(query)
            out_parts.append(out)
        for part, left, right in (
            (slice(0, HEAD), score_parts, query_parts),
            (slice(HEAD, 2 * HEAD), probs_parts, out_parts),
        ):
            left, right = jnp.concatenate(left, axis=1), jnp.concatenate(right, axis=0)
            grads[visible, part] += jnp.dot(left, right, preferred_element_type=F32)
    for rows, target in ((other_rows, send), (own_rows, keep)):
        target[:, :HEAD] = grads[rows, :HEAD] * SCALE
        target[:, HEAD:] = grads[rows, HEAD:]


def attention(*args):
    return call(
        "attention",
        attention_body,
        [((HALF, 2 * HEAD), F32)] * 2,
        args,
        scratch=[pltpu.VMEM((TOK, 2 * HEAD), BF), pltpu.VMEM((TOK, 2 * HEAD), F32)],
        mib=24,
    )


def scale_body(place, keep, recv, key_scale, value_scale, low):
    sequences = own_sequences(place)
    for part, scale in enumerate((key_scale, value_scale)):
        columns = slice(part * HEAD, (part + 1) * HEAD)
        grad = keep[:, columns] + recv[:, columns]
        low[:, columns] = (grad * token_factor(place, scale, sequences)).astype(BF)


def scale_grads(*args):
    return call("scale_grads", scale_body, [((HALF, 2 * HEAD), BF)], args)[0]


def table_body(place, keep, send, base, base_other, sums):
    width = 2 * HEAD
    totals = [jnp.zeros((1, width), F32)] * (SEQS + 1)
    for half, grad, values in ((place[0], keep, base), (1 - place[0], send, base_other)):
        product = grad[...] * values[...]
        row = lax.broadcasted_iota(jnp.int32, product.shape, 0) + half * HALF
        totals[0] += jnp.sum(product, axis=0, keepdims=True)
        for seq in range(1, SEQS):
            later = jnp.where(row >= place[1 + seq], product, 0.0)
            totals[seq] += jnp.sum(later, axis=0, keepdims=True)
    tenant = lax.broadcasted_iota(jnp.int32, sums.shape, 0)
    table = jnp.zeros(sums.shape, F32)
    for seq in range(SEQS):
        table += jnp.where(tenant == place[5 + seq], totals[seq] - totals[seq + 1], 0.0)
    sums[...] = table


def tenant_table(*args):
    return call("tenant_table", table_body, [((NT, 2 * HEAD), F32)], args, mib=8)[0]


def order_body(key_weight, value_weight, out):
    chip = lax.div(lax.axis_index("tensor"), 2)
    for index, (across, row) in enumerate(ORDER):
        columns = pl.ds(pl.multiple_of(home_of(chip, across, row) * HEAD, HEAD), HEAD)
        start = 2 * index * HEAD
        out[:, start : start + HEAD] = key_weight[:, columns]
        out[:, start + HEAD : start + 2 * HEAD] = value_weight[:, columns]


def order_weights(key_weight, value_weight):
    features, depth = key_weight.shape
    outs = [((features, 2 * depth), BF)]
    return call("order_weights", order_body, outs, [key_weight, value_weight])[0]


def place_rows(place, left, mine, other):
    for half, pieces in ((place[0], mine), (1 - place[0], other)):
        rows = pl.ds(pl.multiple_of(half * HALF, HALF), HALF)
        chunks = [piece[row] for piece in pieces for row in range(piece.shape[0])]
        for index, chunk in enumerate(chunks):
            left[rows, 2 * index * HEAD : 2 * (index + 1) * HEAD] = chunk


def near_body(place, mine, mine_far, other, other_far, weight, out, left):
    place_rows(place, left, [mine, mine_far], [other, other_far])
    out[...] = contract_last(left[...], weight[:, : left.shape[1]])


def near_grads(place, mine, other, weight):
    features = weight.shape[0]
    scratch = [pltpu.VMEM((TOK, 6 * HEAD), BF)]
    outs = [((TOK, features), F32)]
    flops = 2 * TOK * features * 6 * HEAD
    args = [place, *mine, *other, weight]
    return call("near_grads", near_body, outs, args, scratch, 8, flops)[0]


def far_half(half, pieces, near, weight, columns):
    chunks = [piece[row] for piece in pieces for row in range(piece.shape[0])]
    left = jnp.concatenate(chunks, axis=1)
    rows = pl.ds(pl.multiple_of(half * HALF, HALF), HALF)
    right = weight[columns, weight.shape[1] - left.shape[1] :]
    return (near[rows, columns] + contract_last(left, right)).astype(BF)


def far_own_body(place, *refs):
    pieces, (near, weight, out) = refs[:-3], refs[-3:]
    steps = 4
    width = out.shape[1] // steps
    for step in range(steps):
        columns = pl.ds(step * width, width)
        out[:, columns] = far_half(place[0], pieces, near, weight, columns)


def far_own(place, pieces, near, weight):
    outs = [((HALF, weight.shape[0]), BF)]
    flops = 2 * HALF * weight.shape[0] * 10 * HEAD
    return call("far_own", far_own_body, outs, [place, *pieces, near, weight], (), 12, flops)[0]


def far_body(place, *refs):
    pieces, (own, near, weight, out, totals, sems) = refs[:-6], refs[-6:]
    own_rows, other_rows = [
        pl.ds(pl.multiple_of(half * HALF, HALF), HALF) for half in (place[0], 1 - place[0])
    ]
    steps, width = totals.shape[0], totals.shape[2]
    writes = [pltpu.make_async_copy(own, out.at[own_rows, :], sems.at[steps])]
    writes[0].start()
    for step in range(steps):
        columns = pl.ds(step * width, width)
        totals[step] = far_half(1 - place[0], pieces, near, weight, columns)
        target = out.at[other_rows, columns]
        writes.append(pltpu.make_async_copy(totals.at[step], target, sems.at[step]))
        writes[-1].start()
    for write in writes:
        write.wait()


def far_grads(place, pieces, own, near, weight):
    features = weight.shape[0]
    steps = 4
    scratch = [
        pltpu.VMEM((steps, HALF, features // steps), BF),
        pltpu.SemaphoreType.DMA((steps + 1,)),
    ]
    outs = [((TOK, features), BF)]
    args = [place, *pieces, own, near, weight]
    flops = 2 * HALF * features * 10 * HEAD
    return call("far_grads", far_body, outs, args, scratch, 12, flops, out_space=pltpu.HBM)[0]


def add_body(*refs):
    total = refs[0][...]
    for ref in refs[1:-1]:
        total = total + ref[...]
    refs[-1][...] = total


def add_up(*parts):
    return call("add_up", add_body, [(parts[0].shape, F32)], parts, mib=4)[0]


def pair_body(mine, other, out):
    out[0] = mine[...]
    out[1] = other[...]


def pair_up(mine, other):
    return call("pair", pair_body, [((2,) + mine.shape, BF)], [mine, other], mib=4)[0]


def own_core():
    return lax.rem(lax.axis_index("tensor"), 2)


def ring_body(here, direct, swapped, three, give):
    total = here[...] + direct[...]
    full = total + swapped[...]
    three[...] = full
    give[...] = jnp.where(own_core() == 0, full, total)


def ring_sums(*parts):
    return call("ring_sums", ring_body, [(parts[0].shape, F32)] * 2, parts, mib=4)


def ring_end_body(three, recv, out):
    out[...] = jnp.where(own_core() == 0, three[...], 0.0) + recv[...]


def ring_end(*parts):
    return call("ring_end", ring_end_body, [(parts[0].shape, F32)], parts, mib=4)[0]


def total_body(here, recv, key, value):
    total = here[...] + recv[...]
    own = lax.broadcasted_iota(jnp.int32, (NT, HEAD // 2), 1) >= 0
    own = own & (own_core() == 0)
    key[...] = jnp.where(own, total[:, : HEAD // 2], total[:, HEAD // 2 : HEAD])
    value[...] = jnp.where(own, total[:, HEAD : HEAD + HEAD // 2], total[:, HEAD + HEAD // 2 :])


def tenant_totals(here, recv):
    return pl.pallas_call(
        total_body,
        out_shape=[jax.ShapeDtypeStruct((NT, HEAD // 2), F32)] * 2,
        compiler_params=pltpu.CompilerParams(vmem_limit_bytes=4 * MIB),
        name="tenant_totals",
    )(here, recv)


def core_swap(array):
    return lax.ppermute(array, "tensor", CORE_SWAP)


def chip_from(array, across, row):
    if across == row == 0:
        return array
    pairs = tensor_pairs(lambda x, y, core: (x - across, y ^ row, core))
    return lax.ppermute(array, "tensor", pairs)


def depth_from(array, steps):
    pairs = []
    for z in range(8):
        for row in range(2):
            for chip in range(CHIPS):
                for core in range(2):
                    source = (z + steps[core]) % 8 * 2 + row
                    place = chip * 2 + core
                    pairs.append((source * 16 + place, (z * 2 + row) * 16 + place))
    return lax.ppermute(array, ("dp", "tensor"), pairs)


def on_device(
    tokens,
    queries,
    out_grad,
    key_weight,
    value_weight,
    key_scale,
    value_scale,
    segment_ids,
    tenant_ids,
):
    place = find_place(segment_ids, tenant_ids)
    key_send, tokens, key_weight, value_weight = load_project(tokens, key_weight, value_weight)
    key_recv = core_swap(key_send)
    value_send = project("project_value", True, tokens, [value_weight], [BF])[0]
    value_recv = core_swap(value_send)
    weights = [key_weight, value_weight]
    key_keep, value_keep = project("project_keep", False, tokens, weights, [F32, F32])
    packed = pack(key_keep, value_keep, key_recv, value_recv)
    part_21, part_11, part_31, part_10, part_30, kept_20, kept_01, kept_00 = packed
    part_20 = relay(kept_20, chip_from(part_21, 0, 1))
    part_01 = relay(kept_01, chip_from(part_11, -1, 0), chip_from(part_31, 1, 0))
    parts = [
        chip_from(part_10, -1, 0),
        chip_from(part_30, 1, 0),
        chip_from(part_20, 2, 0),
        chip_from(part_01, 0, 1),
    ]
    weight = order_weights(key_weight, value_weight)
    parts, weight, place = lax.optimization_barrier((parts, weight, place))
    base, low = finish(place, kept_00, *parts, key_scale, value_scale)
    low_other = core_swap(low)
    base_other = core_swap(base)
    send, keep = attention(place, low, low_other, queries, out_grad)
    recv = core_swap(send)
    sums = tenant_table(place, keep, send, base, base_other)
    recv, sums = lax.optimization_barrier((recv, sums))
    grad_low = scale_grads(place, keep, recv, key_scale, value_scale)
    grad_low, sums_other = lax.optimization_barrier((grad_low, core_swap(sums)))
    sums = add_up(sums, sums_other)
    row_part, far_part, ring = lax.optimization_barrier(
        (chip_from(grad_low, 0, 1), chip_from(grad_low, 2, 0), depth_from(sums, (-1, 1)))
    )
    pair = pair_up(grad_low, row_part)
    three, give = ring_sums(sums, ring, core_swap(ring))
    early = [pair, far_part[None]]
    near = near_grads(place, early, [core_swap(piece) for piece in early], weight)
    arrived = [chip_from(pair, 1, 0), chip_from(pair, 3, 0), chip_from(far_part, 0, 1)]
    arrived, ring, near = lax.optimization_barrier((arrived, depth_from(give, (3, -3)), near))
    arrived = arrived[:2] + [arrived[2][None]]
    sums = ring_end(three, ring)
    own_half = far_own(place, arrived, near, weight)
    others, sums_other, own_half = lax.optimization_barrier(
        ([core_swap(piece) for piece in arrived], core_swap(sums), own_half)
    )
    sums = add_up(sums, sums_other)
    row_sums = lax.ppermute(sums, "dp", [(i, i ^ 1) for i in range(16)])
    input_grad = far_grads(place, others, own_half, near, weight)
    input_grad, row_sums = lax.optimization_barrier((input_grad, row_sums))
    key_total, value_total = tenant_totals(sums, row_sums)
    return input_grad, key_total, value_total


def solution(mesh):
    return jax.shard_map(
        on_device,
        mesh=mesh,
        in_specs=(
            P("dp", "tensor"),
            P("dp", "tensor"),
            P("dp", "tensor"),
            P("tensor", None),
            P("tensor", None),
            P(),
            P(),
            P("dp", None),
            P("dp", None),
        ),
        out_specs=(P("dp", "tensor"), P(None, "tensor"), P(None, "tensor")),
        check_vma=False,
    )
```

```python
import functools

import jax
import jax.numpy as jnp
from jax import lax
from jax.experimental import pallas as pl
from jax.experimental.pallas import tpu as pltpu
from jax.sharding import PartitionSpec as P

SEQS = 4
NT = 32
HEAD = 128
TOK = 512
HALF = 256
CHIPS = 8
BLOCK = 128
LOG2E = 1.4426950408889634
SCALE = HEAD**-0.5
BF = jnp.bfloat16
F32 = jnp.float32
MIB = 1024 * 1024


def call(name, body, outs, args, scratch=(), mib=16, flops=0, out_space=pltpu.VMEM):
    spaces = [pltpu.SMEM if array.ndim == 1 else pltpu.VMEM for array in args]
    placed = [
        array if space is pltpu.SMEM else pltpu.with_memory_space_constraint(array, space)
        for array, space in zip(args, spaces)
    ]
    nbytes = sum(array.size * array.dtype.itemsize for array in args)
    return pl.pallas_call(
        body,
        in_specs=[pl.BlockSpec(memory_space=space) for space in spaces],
        out_specs=[pl.BlockSpec(memory_space=out_space)] * len(outs),
        out_shape=[out_space(*out) for out in outs],
        scratch_shapes=list(scratch),
        compiler_params=pltpu.CompilerParams(vmem_limit_bytes=mib * MIB),
        cost_estimate=pl.CostEstimate(flops=flops, bytes_accessed=nbytes, transcendentals=0),
        name=name,
    )(*placed)


def device_index(x, y, core):
    return (x % 4 * 2 + y) * 2 + core


def tensor_pairs(step):
    places = [(x, y, core) for x in range(4) for y in range(2) for core in range(2)]
    return [(device_index(*place), device_index(*step(*place))) for place in places]


CORE_SWAP = tensor_pairs(lambda x, y, core: (x, y, core ^ 1))
ORDER = [(0, 0), (0, 1), (2, 0), (1, 0), (1, 1), (3, 0), (3, 1), (2, 1)]
SENT = [(2, 1), (1, 1), (3, 1), (1, 0), (3, 0)]
KEPT = [(2, 0), (0, 1), (0, 0)]


def load_body(tokens, key_weight, value_weight, send, rows, key_out, value_out, sems):
    core = lax.rem(lax.axis_index("tensor"), 2)
    halves = [pl.ds(pl.multiple_of(half * HALF, HALF), HALF) for half in (1 - core, core)]
    steps = 4
    width = send.shape[1] // steps
    chunks = [pl.ds(step * width, width) for step in range(steps)]
    pairs = [(tokens.at[halves[0], :], rows.at[halves[0], :])]
    pairs += [(key_weight.at[:, chunk], key_out.at[:, chunk]) for chunk in chunks]
    pairs += [(tokens.at[halves[1], :], rows.at[halves[1], :]), (value_weight, value_out)]
    copies = [pltpu.make_async_copy(*pair, sems.at[i]) for i, pair in enumerate(pairs)]
    for copy in copies:
        copy.start()
    copies[0].wait()
    for chunk, copy in zip(chunks, copies[1:]):
        copy.wait()
        send[:, chunk] = jnp.dot(
            rows[halves[0], :], key_out[:, chunk], preferred_element_type=F32
        )
    for copy in copies[steps + 1 :]:
        copy.wait()


def load_project(tokens, key_weight, value_weight):
    args = [pltpu.with_memory_space_constraint(x, pltpu.HBM) for x in (tokens, key_weight, value_weight)]
    outs = [((HALF, CHIPS * HEAD), F32)] + [(x.shape, BF) for x in args]
    return pl.pallas_call(
        load_body,
        in_specs=[pl.BlockSpec(memory_space=pltpu.HBM)] * 3,
        out_specs=[pl.BlockSpec(memory_space=pltpu.VMEM)] * 4,
        out_shape=[pltpu.VMEM(*out) for out in outs],
        scratch_shapes=[pltpu.SemaphoreType.DMA((7,))],
        compiler_params=pltpu.CompilerParams(vmem_limit_bytes=16 * MIB),
        name="project_key",
    )(*args)


def home_of(chip, across, row):
    home = lax.rem(chip + 2 * across, CHIPS)
    return home + row * (1 - 2 * lax.rem(home, 2))


def project_body(flip, count, tokens, *refs):
    weights, outs = refs[:count], refs[count:]
    core = lax.rem(lax.axis_index("tensor"), 2)
    half = 1 - core if flip else core
    rows = pl.ds(pl.multiple_of(half * HALF, HALF), HALF)
    for weight, out in zip(weights, outs):
        out[...] = jnp.dot(tokens[rows, :], weight[...], preferred_element_type=F32).astype(out.dtype)


def project(name, flip, tokens, weights, dtypes):
    depth, columns = weights[0].shape
    count = len(weights)
    return call(
        name,
        functools.partial(project_body, flip, count),
        [((HALF, columns), dtype) for dtype in dtypes],
        [tokens, *weights],
        flops=2 * count * HALF * depth * columns,
    )


def encode(total, out):
    high = total[:, :HEAD].astype(BF)
    out[:, :HEAD] = high
    out[:, HEAD : 2 * HEAD] = (total[:, :HEAD] - high.astype(F32)).astype(BF)
    out[:, 2 * HEAD :] = total[:, HEAD:].astype(BF)


def decode(part):
    key = part[:, :HEAD].astype(F32) + part[:, HEAD : 2 * HEAD].astype(F32)
    return jnp.concatenate([key, part[:, 2 * HEAD :].astype(F32)], axis=1)


def pack_body(chunks, key_keep, value_keep, key_recv, value_recv, *outs):
    chip = lax.div(lax.axis_index("tensor"), 2)
    for (across, row), out in zip(chunks, outs):
        columns = pl.ds(pl.multiple_of(home_of(chip, across, row) * HEAD, HEAD), HEAD)
        key = key_keep[:, columns] + key_recv[:, columns]
        value = value_keep[:, columns] + value_recv[:, columns].astype(F32)
        total = jnp.concatenate([key, value], axis=1)
        if (across, row) in KEPT:
            out[...] = total
        else:
            encode(total, out)


def pack(name, chunks, *parts):
    outs = [
        ((HALF, 2 * HEAD), F32) if chunk in KEPT else ((HALF, 3 * HEAD), BF) for chunk in chunks
    ]
    return call(name, functools.partial(pack_body, chunks), outs, parts)


def relay_body(kept, *refs):
    total = kept[...]
    for part in refs[:-1]:
        total = total + decode(part[...])
    encode(total, refs[-1])


def relay(*parts):
    return call("relay", relay_body, [((HALF, 3 * HEAD), BF)], parts, mib=8)[0]


def place_body(segments, tenants, place):
    rank = lax.axis_index("tensor")
    place[0] = lax.rem(rank, 2)
    for seq in range(SEQS):
        place[1 + seq] = jnp.sum((segments[...] < seq).astype(jnp.int32))
        place[5 + seq] = tenants[0, seq]
    place[9] = lax.div(rank, 2)


def find_place(segment_ids, tenant_ids):
    smem = pl.BlockSpec(memory_space=pltpu.SMEM)
    return pl.pallas_call(
        place_body,
        in_specs=[pl.BlockSpec(memory_space=pltpu.VMEM), smem],
        out_specs=smem,
        out_shape=jax.ShapeDtypeStruct((10,), jnp.int32),
        compiler_params=pltpu.CompilerParams(vmem_limit_bytes=4 * MIB),
        name="place",
    )(segment_ids, tenant_ids)


def own_sequences(place):
    row = lax.broadcasted_iota(jnp.int32, (HALF, HEAD), 0) + place[0] * HALF
    found = [row >= place[1 + seq] for seq in range(1, SEQS)]
    return found


def token_factor(place, scale, sequences):
    columns = pl.ds(pl.multiple_of(place[9] * HEAD, HEAD), HEAD)
    table = scale[:, columns]
    tenant = lax.broadcasted_iota(jnp.int32, table.shape, 0)
    rows = [
        jnp.sum(jnp.where(tenant == place[5 + seq], table, 0.0), axis=0, keepdims=True)
        for seq in range(SEQS)
    ]
    factor = jnp.broadcast_to(rows[0], (HALF, HEAD))
    for seq in range(1, SEQS):
        factor = jnp.where(sequences[seq - 1], rows[seq], factor)
    return factor


def finish_body(place, kept, *refs):
    parts, (key_scale, value_scale, base, low) = refs[:-4], refs[-4:]
    total = kept[...]
    for part in parts:
        total = total + decode(part[...])
    sequences = own_sequences(place)
    key = total[:, :HEAD]
    value = total[:, HEAD:]
    base[:, :HEAD] = key
    base[:, HEAD:] = value
    low[:, :HEAD] = (key * token_factor(place, key_scale, sequences)).astype(BF)
    low[:, HEAD:] = (value * token_factor(place, value_scale, sequences)).astype(BF)


def finish(*args):
    return call("finish", finish_body, [((HALF, 2 * HEAD), F32), ((HALF, 2 * HEAD), BF)], args)


def contract_last(left, right):
    return lax.dot_general(left, right, (((1,), (1,)), ((), ())), preferred_element_type=F32)


def attention_body(place, mine, other, queries, out_grad, send, keep, tile, grads):
    core = place[0]
    own_rows = pl.ds(pl.multiple_of(core * HALF, HALF), HALF)
    other_rows = pl.ds(pl.multiple_of((1 - core) * HALF, HALF), HALF)
    tile[own_rows, :] = mine[...]
    tile[other_rows, :] = other[...]
    grads[...] = jnp.zeros_like(grads)
    heads = queries.shape[1] // HEAD
    for block in range(TOK // BLOCK):
        first = max(0, block - 2) * BLOCK
        reach = (block + 1) * BLOCK - first
        rows = slice(block * BLOCK, (block + 1) * BLOCK)
        visible = slice(first, first + reach)
        key_row = lax.broadcasted_iota(jnp.int32, (reach, BLOCK), 0) + first
        query_row = lax.broadcasted_iota(jnp.int32, (reach, BLOCK), 1) + block * BLOCK
        start = jnp.zeros((reach, BLOCK), jnp.int32)
        for seq in range(1, SEQS):
            start = jnp.where(query_row >= place[1 + seq], place[1 + seq], start)
        allowed = (key_row >= start) & (key_row <= query_row)
        bias = jnp.where(allowed, 0.0, -1e30).astype(F32)
        bias = jnp.concatenate([bias, bias], axis=1)
        key_tile = tile[visible, :HEAD]
        value_tile = tile[visible, HEAD:]
        probs_parts, score_parts, query_parts, out_parts = [], [], [], []
        for pair in range(heads // 2):
            columns = [slice(h * HEAD, (h + 1) * HEAD) for h in (2 * pair, 2 * pair + 1)]
            query = jnp.concatenate([queries[rows, c] for c in columns], axis=0)
            out = jnp.concatenate([out_grad[rows, c] for c in columns], axis=0)
            scores = contract_last(key_tile, query) + bias
            peak = jnp.max(scores, axis=0, keepdims=True)
            exps = jnp.exp2((scores - peak) * (SCALE * LOG2E))
            probs = exps * (1.0 / jnp.sum(exps, axis=0, keepdims=True))
            probs_low = probs.astype(BF)
            prob_grad = contract_last(value_tile, out)
            delta = jnp.sum(probs_low.astype(F32) * prob_grad, axis=0, keepdims=True)
            score_parts.append((probs * (prob_grad - delta)).astype(BF))
            probs_parts.append(probs_low)
            query_parts.append(query)
            out_parts.append(out)
        for part, left, right in (
            (slice(0, HEAD), score_parts, query_parts),
            (slice(HEAD, 2 * HEAD), probs_parts, out_parts),
        ):
            left, right = jnp.concatenate(left, axis=1), jnp.concatenate(right, axis=0)
            grads[visible, part] += jnp.dot(left, right, preferred_element_type=F32)
    for rows, target in ((other_rows, send), (own_rows, keep)):
        target[:, :HEAD] = grads[rows, :HEAD] * SCALE
        target[:, HEAD:] = grads[rows, HEAD:]


def attention(*args):
    return call(
        "attention",
        attention_body,
        [((HALF, 2 * HEAD), F32)] * 2,
        args,
        scratch=[pltpu.VMEM((TOK, 2 * HEAD), BF), pltpu.VMEM((TOK, 2 * HEAD), F32)],
        mib=24,
    )


def scale_body(place, keep, recv, key_scale, value_scale, low):
    sequences = own_sequences(place)
    for part, scale in enumerate((key_scale, value_scale)):
        columns = slice(part * HEAD, (part + 1) * HEAD)
        grad = keep[:, columns] + recv[:, columns]
        low[:, columns] = (grad * token_factor(place, scale, sequences)).astype(BF)


def scale_grads(*args):
    return call("scale_grads", scale_body, [((HALF, 2 * HEAD), BF)], args)[0]


def table_body(place, keep, send, base, base_other, sums):
    width = 2 * HEAD
    totals = [jnp.zeros((1, width), F32)] * (SEQS + 1)
    for half, grad, values in ((place[0], keep, base), (1 - place[0], send, base_other)):
        product = grad[...] * values[...]
        row = lax.broadcasted_iota(jnp.int32, product.shape, 0) + half * HALF
        totals[0] += jnp.sum(product, axis=0, keepdims=True)
        for seq in range(1, SEQS):
            later = jnp.where(row >= place[1 + seq], product, 0.0)
            totals[seq] += jnp.sum(later, axis=0, keepdims=True)
    tenant = lax.broadcasted_iota(jnp.int32, sums.shape, 0)
    table = jnp.zeros(sums.shape, F32)
    for seq in range(SEQS):
        table += jnp.where(tenant == place[5 + seq], totals[seq] - totals[seq + 1], 0.0)
    sums[...] = table


def tenant_table(*args):
    return call("tenant_table", table_body, [((NT, 2 * HEAD), F32)], args, mib=8)[0]


def order_body(key_weight, value_weight, out):
    chip = lax.div(lax.axis_index("tensor"), 2)
    for index, (across, row) in enumerate(ORDER):
        columns = pl.ds(pl.multiple_of(home_of(chip, across, row) * HEAD, HEAD), HEAD)
        start = 2 * index * HEAD
        out[:, start : start + HEAD] = key_weight[:, columns]
        out[:, start + HEAD : start + 2 * HEAD] = value_weight[:, columns]


def order_weights(key_weight, value_weight):
    features, depth = key_weight.shape
    outs = [((features, 2 * depth), BF)]
    return call("order_weights", order_body, outs, [key_weight, value_weight])[0]


def place_rows(place, left, mine, other):
    for half, pieces in ((place[0], mine), (1 - place[0], other)):
        rows = pl.ds(pl.multiple_of(half * HALF, HALF), HALF)
        chunks = [piece[row] for piece in pieces for row in range(piece.shape[0])]
        for index, chunk in enumerate(chunks):
            left[rows, 2 * index * HEAD : 2 * (index + 1) * HEAD] = chunk


def near_body(place, mine, mine_far, other, other_far, weight, out, left):
    place_rows(place, left, [mine, mine_far], [other, other_far])
    out[...] = contract_last(left[...], weight[:, : left.shape[1]])


def near_grads(place, mine, other, weight):
    features = weight.shape[0]
    scratch = [pltpu.VMEM((TOK, 6 * HEAD), BF)]
    outs = [((TOK, features), F32)]
    flops = 2 * TOK * features * 6 * HEAD
    args = [place, *mine, *other, weight]
    return call("near_grads", near_body, outs, args, scratch, 8, flops)[0]


def far_half(half, pieces, near, weight, columns):
    chunks = [piece[row] for piece in pieces for row in range(piece.shape[0])]
    left = jnp.concatenate(chunks, axis=1)
    rows = pl.ds(pl.multiple_of(half * HALF, HALF), HALF)
    right = weight[columns, weight.shape[1] - left.shape[1] :]
    return (near[rows, columns] + contract_last(left, right)).astype(BF)


def far_own_body(place, *refs):
    pieces, (near, weight, out) = refs[:-3], refs[-3:]
    steps = 4
    width = out.shape[1] // steps
    for step in range(steps):
        columns = pl.ds(step * width, width)
        out[:, columns] = far_half(place[0], pieces, near, weight, columns)


def far_own(place, pieces, near, weight):
    outs = [((HALF, weight.shape[0]), BF)]
    flops = 2 * HALF * weight.shape[0] * 10 * HEAD
    return call("far_own", far_own_body, outs, [place, *pieces, near, weight], (), 12, flops)[0]


def far_body(place, *refs):
    pieces, (own, near, weight, out, totals, sems) = refs[:-6], refs[-6:]
    own_rows, other_rows = [
        pl.ds(pl.multiple_of(half * HALF, HALF), HALF) for half in (place[0], 1 - place[0])
    ]
    steps, width = totals.shape[0], totals.shape[2]
    writes = [pltpu.make_async_copy(own, out.at[own_rows, :], sems.at[steps])]
    writes[0].start()
    for step in range(steps):
        columns = pl.ds(step * width, width)
        totals[step] = far_half(1 - place[0], pieces, near, weight, columns)
        target = out.at[other_rows, columns]
        writes.append(pltpu.make_async_copy(totals.at[step], target, sems.at[step]))
        writes[-1].start()
    for write in writes:
        write.wait()


def far_grads(place, pieces, own, near, weight):
    features = weight.shape[0]
    steps = 4
    scratch = [
        pltpu.VMEM((steps, HALF, features // steps), BF),
        pltpu.SemaphoreType.DMA((steps + 1,)),
    ]
    outs = [((TOK, features), BF)]
    args = [place, *pieces, own, near, weight]
    flops = 2 * HALF * features * 10 * HEAD
    return call("far_grads", far_body, outs, args, scratch, 12, flops, out_space=pltpu.HBM)[0]


def add_body(*refs):
    total = refs[0][...]
    for ref in refs[1:-1]:
        total = total + ref[...]
    refs[-1][...] = total


def add_up(*parts):
    return call("add_up", add_body, [(parts[0].shape, F32)], parts, mib=4)[0]


def pair_body(mine, other, out):
    out[0] = mine[...]
    out[1] = other[...]


def pair_up(mine, other):
    return call("pair", pair_body, [((2,) + mine.shape, BF)], [mine, other], mib=4)[0]


def own_core():
    return lax.rem(lax.axis_index("tensor"), 2)


def ring_body(here, direct, swapped, three, give):
    total = here[...] + direct[...]
    full = total + swapped[...]
    three[...] = full
    give[...] = jnp.where(own_core() == 0, full, total)


def ring_sums(*parts):
    return call("ring_sums", ring_body, [(parts[0].shape, F32)] * 2, parts, mib=4)


def ring_end_body(three, recv, out):
    out[...] = jnp.where(own_core() == 0, three[...], 0.0) + recv[...]


def ring_end(*parts):
    return call("ring_end", ring_end_body, [(parts[0].shape, F32)], parts, mib=4)[0]


def total_body(here, recv, key, value):
    total = here[...] + recv[...]
    own = lax.broadcasted_iota(jnp.int32, (NT, HEAD // 2), 1) >= 0
    own = own & (own_core() == 0)
    key[...] = jnp.where(own, total[:, : HEAD // 2], total[:, HEAD // 2 : HEAD])
    value[...] = jnp.where(own, total[:, HEAD : HEAD + HEAD // 2], total[:, HEAD + HEAD // 2 :])


def tenant_totals(here, recv):
    return pl.pallas_call(
        total_body,
        out_shape=[jax.ShapeDtypeStruct((NT, HEAD // 2), F32)] * 2,
        compiler_params=pltpu.CompilerParams(vmem_limit_bytes=4 * MIB),
        name="tenant_totals",
    )(here, recv)


def core_swap(array):
    return lax.ppermute(array, "tensor", CORE_SWAP)


def chip_from(array, across, row):
    if across == row == 0:
        return array
    pairs = tensor_pairs(lambda x, y, core: (x - across, y ^ row, core))
    return lax.ppermute(array, "tensor", pairs)


def depth_from(array, steps):
    pairs = []
    for z in range(8):
        for row in range(2):
            for chip in range(CHIPS):
                for core in range(2):
                    source = (z + steps[core]) % 8 * 2 + row
                    place = chip * 2 + core
                    pairs.append((source * 16 + place, (z * 2 + row) * 16 + place))
    return lax.ppermute(array, ("dp", "tensor"), pairs)


def on_device(
    tokens,
    queries,
    out_grad,
    key_weight,
    value_weight,
    key_scale,
    value_scale,
    segment_ids,
    tenant_ids,
):
    place = find_place(segment_ids, tenant_ids)
    key_send, tokens, key_weight, value_weight = load_project(tokens, key_weight, value_weight)
    key_recv = core_swap(key_send)
    value_send = project("project_value", True, tokens, [value_weight], [BF])[0]
    value_recv = core_swap(value_send)
    weights = [key_weight, value_weight]
    key_keep, value_keep = project("project_keep", False, tokens, weights, [F32, F32])
    sides = (key_keep, value_keep, key_recv, value_recv)
    part_21, part_11, part_31 = pack("pack_relayed", SENT[:3], *sides)
    part_10, part_30, kept_20, kept_01, kept_00 = pack("pack_rest", SENT[3:] + KEPT, *sides)
    part_20 = relay(kept_20, chip_from(part_21, 0, 1))
    part_01 = relay(kept_01, chip_from(part_11, -1, 0), chip_from(part_31, 1, 0))
    parts = [
        chip_from(part_10, -1, 0),
        chip_from(part_30, 1, 0),
        chip_from(part_20, 2, 0),
        chip_from(part_01, 0, 1),
    ]
    weight = order_weights(key_weight, value_weight)
    parts, weight, place = lax.optimization_barrier((parts, weight, place))
    base, low = finish(place, kept_00, *parts, key_scale, value_scale)
    low_other = core_swap(low)
    base_other = core_swap(base)
    send, keep = attention(place, low, low_other, queries, out_grad)
    recv = core_swap(send)
    sums = tenant_table(place, keep, send, base, base_other)
    recv, sums = lax.optimization_barrier((recv, sums))
    grad_low = scale_grads(place, keep, recv, key_scale, value_scale)
    grad_low, sums_other = lax.optimization_barrier((grad_low, core_swap(sums)))
    sums = add_up(sums, sums_other)
    row_part, ring = lax.optimization_barrier(
        (chip_from(grad_low, 0, 1), depth_from(sums, (-1, 1)))
    )
    pair, far_part = lax.optimization_barrier(
        (pair_up(grad_low, row_part), chip_from(grad_low, 2, 0))
    )
    three, give = ring_sums(sums, ring, core_swap(ring))
    early = [pair, far_part[None]]
    near = near_grads(place, early, [core_swap(piece) for piece in early], weight)
    arrived = [chip_from(pair, 1, 0), chip_from(pair, 3, 0), chip_from(far_part, 0, 1)]
    arrived, ring, near = lax.optimization_barrier((arrived, depth_from(give, (3, -3)), near))
    arrived = arrived[:2] + [arrived[2][None]]
    sums = ring_end(three, ring)
    own_half = far_own(place, arrived, near, weight)
    others, sums_other, own_half = lax.optimization_barrier(
        ([core_swap(piece) for piece in arrived], core_swap(sums), own_half)
    )
    sums = add_up(sums, sums_other)
    row_sums = lax.ppermute(sums, "dp", [(i, i ^ 1) for i in range(16)])
    input_grad = far_grads(place, others, own_half, near, weight)
    input_grad, row_sums = lax.optimization_barrier((input_grad, row_sums))
    key_total, value_total = tenant_totals(sums, row_sums)
    return input_grad, key_total, value_total


def solution(mesh):
    return jax.shard_map(
        on_device,
        mesh=mesh,
        in_specs=(
            P("dp", "tensor"),
            P("dp", "tensor"),
            P("dp", "tensor"),
            P("tensor", None),
            P("tensor", None),
            P(),
            P(),
            P("dp", None),
            P("dp", None),
        ),
        out_specs=(P("dp", "tensor"), P(None, "tensor"), P(None, "tensor")),
        check_vma=False,
    )
```

```python
import functools

import jax
import jax.numpy as jnp
from jax import lax
from jax.experimental import pallas as pl
from jax.experimental.pallas import tpu as pltpu
from jax.sharding import PartitionSpec as P

SEQS = 4
NT = 32
HEAD = 128
TOK = 512
HALF = 256
CHIPS = 8
BLOCK = 128
LOG2E = 1.4426950408889634
SCALE = HEAD**-0.5
BF = jnp.bfloat16
F32 = jnp.float32
MIB = 1024 * 1024


def call(name, body, outs, args, scratch=(), mib=16, flops=0, out_space=pltpu.VMEM):
    spaces = [pltpu.SMEM if array.ndim == 1 else pltpu.VMEM for array in args]
    placed = [
        array if space is pltpu.SMEM else pltpu.with_memory_space_constraint(array, space)
        for array, space in zip(args, spaces)
    ]
    nbytes = sum(array.size * array.dtype.itemsize for array in args)
    return pl.pallas_call(
        body,
        in_specs=[pl.BlockSpec(memory_space=space) for space in spaces],
        out_specs=[pl.BlockSpec(memory_space=out_space)] * len(outs),
        out_shape=[out_space(*out) for out in outs],
        scratch_shapes=list(scratch),
        compiler_params=pltpu.CompilerParams(vmem_limit_bytes=mib * MIB),
        cost_estimate=pl.CostEstimate(flops=flops, bytes_accessed=nbytes, transcendentals=0),
        name=name,
    )(*placed)


def device_index(x, y, core):
    return (x % 4 * 2 + y) * 2 + core


def tensor_pairs(step):
    places = [(x, y, core) for x in range(4) for y in range(2) for core in range(2)]
    return [(device_index(*place), device_index(*step(*place))) for place in places]


CORE_SWAP = tensor_pairs(lambda x, y, core: (x, y, core ^ 1))
ORDER = [(0, 0), (0, 1), (2, 0), (1, 0), (1, 1), (3, 0), (3, 1), (2, 1)]
SENT = [(2, 1), (1, 1), (3, 1), (1, 0), (3, 0)]
KEPT = [(2, 0), (0, 1), (0, 0)]


def load_body(tokens, key_weight, value_weight, send, rows, key_out, value_out, sems):
    core = lax.rem(lax.axis_index("tensor"), 2)
    halves = [pl.ds(pl.multiple_of(half * HALF, HALF), HALF) for half in (1 - core, core)]
    steps = 4
    width = send.shape[1] // steps
    chunks = [pl.ds(step * width, width) for step in range(steps)]
    pairs = [(tokens.at[halves[0], :], rows.at[halves[0], :])]
    pairs += [(key_weight.at[:, chunk], key_out.at[:, chunk]) for chunk in chunks]
    pairs += [(tokens.at[halves[1], :], rows.at[halves[1], :]), (value_weight, value_out)]
    copies = [pltpu.make_async_copy(*pair, sems.at[i]) for i, pair in enumerate(pairs)]
    for copy in copies:
        copy.start()
    copies[0].wait()
    for chunk, copy in zip(chunks, copies[1:]):
        copy.wait()
        send[:, chunk] = jnp.dot(
            rows[halves[0], :], key_out[:, chunk], preferred_element_type=F32
        )
    for copy in copies[steps + 1 :]:
        copy.wait()


def load_project(tokens, key_weight, value_weight):
    args = [pltpu.with_memory_space_constraint(x, pltpu.HBM) for x in (tokens, key_weight, value_weight)]
    outs = [((HALF, CHIPS * HEAD), F32)] + [(x.shape, BF) for x in args]
    return pl.pallas_call(
        load_body,
        in_specs=[pl.BlockSpec(memory_space=pltpu.HBM)] * 3,
        out_specs=[pl.BlockSpec(memory_space=pltpu.VMEM)] * 4,
        out_shape=[pltpu.VMEM(*out) for out in outs],
        scratch_shapes=[pltpu.SemaphoreType.DMA((7,))],
        compiler_params=pltpu.CompilerParams(vmem_limit_bytes=16 * MIB),
        name="project_key",
    )(*args)


def home_of(chip, across, row):
    home = lax.rem(chip + 2 * across, CHIPS)
    return home + row * (1 - 2 * lax.rem(home, 2))


def project_body(flip, count, tokens, *refs):
    weights, outs = refs[:count], refs[count:]
    core = lax.rem(lax.axis_index("tensor"), 2)
    half = 1 - core if flip else core
    rows = pl.ds(pl.multiple_of(half * HALF, HALF), HALF)
    for weight, out in zip(weights, outs):
        out[...] = jnp.dot(tokens[rows, :], weight[...], preferred_element_type=F32).astype(out.dtype)


def project(name, flip, tokens, weights, dtypes):
    depth, columns = weights[0].shape
    count = len(weights)
    return call(
        name,
        functools.partial(project_body, flip, count),
        [((HALF, columns), dtype) for dtype in dtypes],
        [tokens, *weights],
        flops=2 * count * HALF * depth * columns,
    )


def encode(total, out):
    high = total[:, :HEAD].astype(BF)
    out[:, :HEAD] = high
    out[:, HEAD : 2 * HEAD] = (total[:, :HEAD] - high.astype(F32)).astype(BF)
    out[:, 2 * HEAD :] = total[:, HEAD:].astype(BF)


def decode(part):
    key = part[:, :HEAD].astype(F32) + part[:, HEAD : 2 * HEAD].astype(F32)
    return jnp.concatenate([key, part[:, 2 * HEAD :].astype(F32)], axis=1)


def pack_body(chunks, key_keep, value_keep, key_recv, value_recv, *outs):
    chip = lax.div(lax.axis_index("tensor"), 2)
    for (across, row), out in zip(chunks, outs):
        columns = pl.ds(pl.multiple_of(home_of(chip, across, row) * HEAD, HEAD), HEAD)
        key = key_keep[:, columns] + key_recv[:, columns]
        value = value_keep[:, columns] + value_recv[:, columns].astype(F32)
        total = jnp.concatenate([key, value], axis=1)
        if (across, row) in KEPT:
            out[...] = total
        else:
            encode(total, out)


def pack(name, chunks, *parts):
    outs = [
        ((HALF, 2 * HEAD), F32) if chunk in KEPT else ((HALF, 3 * HEAD), BF) for chunk in chunks
    ]
    return call(name, functools.partial(pack_body, chunks), outs, parts)


def relay_body(kept, *refs):
    total = kept[...]
    for part in refs[:-1]:
        total = total + decode(part[...])
    encode(total, refs[-1])


def relay(*parts):
    return call("relay", relay_body, [((HALF, 3 * HEAD), BF)], parts, mib=8)[0]


def place_body(segments, tenants, place):
    rank = lax.axis_index("tensor")
    place[0] = lax.rem(rank, 2)
    for seq in range(SEQS):
        place[1 + seq] = jnp.sum((segments[...] < seq).astype(jnp.int32))
        place[5 + seq] = tenants[0, seq]
    place[9] = lax.div(rank, 2)


def find_place(segment_ids, tenant_ids):
    smem = pl.BlockSpec(memory_space=pltpu.SMEM)
    return pl.pallas_call(
        place_body,
        in_specs=[pl.BlockSpec(memory_space=pltpu.VMEM), smem],
        out_specs=smem,
        out_shape=jax.ShapeDtypeStruct((10,), jnp.int32),
        compiler_params=pltpu.CompilerParams(vmem_limit_bytes=4 * MIB),
        name="place",
    )(segment_ids, tenant_ids)


def own_sequences(place):
    row = lax.broadcasted_iota(jnp.int32, (HALF, HEAD), 0) + place[0] * HALF
    found = [row >= place[1 + seq] for seq in range(1, SEQS)]
    return found


def token_factor(place, scale, sequences):
    columns = pl.ds(pl.multiple_of(place[9] * HEAD, HEAD), HEAD)
    table = scale[:, columns]
    tenant = lax.broadcasted_iota(jnp.int32, table.shape, 0)
    rows = [
        jnp.sum(jnp.where(tenant == place[5 + seq], table, 0.0), axis=0, keepdims=True)
        for seq in range(SEQS)
    ]
    factor = jnp.broadcast_to(rows[0], (HALF, HEAD))
    for seq in range(1, SEQS):
        factor = jnp.where(sequences[seq - 1], rows[seq], factor)
    return factor


def finish_body(place, kept, *refs):
    parts, (key_scale, value_scale, base, low) = refs[:-4], refs[-4:]
    total = kept[...]
    for part in parts:
        total = total + decode(part[...])
    sequences = own_sequences(place)
    key = total[:, :HEAD]
    value = total[:, HEAD:]
    base[:, :HEAD] = key
    base[:, HEAD:] = value
    low[:, :HEAD] = (key * token_factor(place, key_scale, sequences)).astype(BF)
    low[:, HEAD:] = (value * token_factor(place, value_scale, sequences)).astype(BF)


def finish(*args):
    return call("finish", finish_body, [((HALF, 2 * HEAD), F32), ((HALF, 2 * HEAD), BF)], args)


def contract_last(left, right):
    return lax.dot_general(left, right, (((1,), (1,)), ((), ())), preferred_element_type=F32)


def attention_body(place, mine, other, queries, out_grad, send, keep, tile, grads):
    core = place[0]
    own_rows = pl.ds(pl.multiple_of(core * HALF, HALF), HALF)
    other_rows = pl.ds(pl.multiple_of((1 - core) * HALF, HALF), HALF)
    tile[own_rows, :] = mine[...]
    tile[other_rows, :] = other[...]
    heads = queries.shape[1] // HEAD
    for block in range(TOK // BLOCK):
        first = max(0, block - 2) * BLOCK
        reach = (block + 1) * BLOCK - first
        rows = slice(block * BLOCK, (block + 1) * BLOCK)
        visible = slice(first, first + reach)
        key_row = lax.broadcasted_iota(jnp.int32, (reach, BLOCK), 0) + first
        query_row = lax.broadcasted_iota(jnp.int32, (1, BLOCK), 1) + block * BLOCK
        start = jnp.zeros((1, BLOCK), jnp.int32)
        for seq in range(1, SEQS):
            start = jnp.where(query_row >= place[1 + seq], place[1 + seq], start)
        allowed = (key_row >= start) & (key_row <= query_row)
        bias = jnp.where(allowed, 0.0, -1e30).astype(F32)
        bias = jnp.concatenate([bias, bias], axis=1)
        key_tile = tile[visible, :HEAD]
        value_tile = tile[visible, HEAD:]
        probs_parts, score_parts, query_parts, out_parts = [], [], [], []
        for pair in range(heads // 2):
            columns = [slice(h * HEAD, (h + 1) * HEAD) for h in (2 * pair, 2 * pair + 1)]
            query = jnp.concatenate([queries[rows, c] for c in columns], axis=0)
            out = jnp.concatenate([out_grad[rows, c] for c in columns], axis=0)
            scores = contract_last(key_tile, query) + bias
            peak = jnp.max(scores, axis=0, keepdims=True)
            exps = jnp.exp2((scores - peak) * (SCALE * LOG2E))
            probs = exps * (1.0 / jnp.sum(exps, axis=0, keepdims=True))
            probs_low = probs.astype(BF)
            prob_grad = contract_last(value_tile, out)
            delta = jnp.sum(probs_low.astype(F32) * prob_grad, axis=0, keepdims=True)
            score_parts.append((probs * (prob_grad - delta)).astype(BF))
            probs_parts.append(probs_low)
            query_parts.append(query)
            out_parts.append(out)
        for part, left, right in (
            (slice(0, HEAD), score_parts, query_parts),
            (slice(HEAD, 2 * HEAD), probs_parts, out_parts),
        ):
            left, right = jnp.concatenate(left, axis=1), jnp.concatenate(right, axis=0)
            total = jnp.dot(left, right, preferred_element_type=F32)
            if reach > BLOCK:
                grads[first : first + reach - BLOCK, part] += total[: reach - BLOCK]
            grads[rows, part] = total[reach - BLOCK :]
    for rows, target in ((other_rows, send), (own_rows, keep)):
        target[:, :HEAD] = grads[rows, :HEAD] * SCALE
        target[:, HEAD:] = grads[rows, HEAD:]


def attention(*args):
    return call(
        "attention",
        attention_body,
        [((HALF, 2 * HEAD), F32)] * 2,
        args,
        scratch=[pltpu.VMEM((TOK, 2 * HEAD), BF), pltpu.VMEM((TOK, 2 * HEAD), F32)],
        mib=24,
    )


def scale_body(place, keep, recv, key_scale, value_scale, low):
    sequences = own_sequences(place)
    for part, scale in enumerate((key_scale, value_scale)):
        columns = slice(part * HEAD, (part + 1) * HEAD)
        grad = keep[:, columns] + recv[:, columns]
        low[:, columns] = (grad * token_factor(place, scale, sequences)).astype(BF)


def scale_grads(*args):
    return call("scale_grads", scale_body, [((HALF, 2 * HEAD), BF)], args)[0]


def table_body(place, keep, send, base, base_other, sums):
    width = 2 * HEAD
    totals = [jnp.zeros((1, width), F32)] * (SEQS + 1)
    for half, grad, values in ((place[0], keep, base), (1 - place[0], send, base_other)):
        product = grad[...] * values[...]
        row = lax.broadcasted_iota(jnp.int32, product.shape, 0) + half * HALF
        totals[0] += jnp.sum(product, axis=0, keepdims=True)
        for seq in range(1, SEQS):
            later = jnp.where(row >= place[1 + seq], product, 0.0)
            totals[seq] += jnp.sum(later, axis=0, keepdims=True)
    tenant = lax.broadcasted_iota(jnp.int32, sums.shape, 0)
    table = jnp.zeros(sums.shape, F32)
    for seq in range(SEQS):
        table += jnp.where(tenant == place[5 + seq], totals[seq] - totals[seq + 1], 0.0)
    sums[...] = table


def tenant_table(*args):
    return call("tenant_table", table_body, [((NT, 2 * HEAD), F32)], args, mib=8)[0]


def order_body(key_weight, value_weight, out):
    chip = lax.div(lax.axis_index("tensor"), 2)
    for index, (across, row) in enumerate(ORDER):
        columns = pl.ds(pl.multiple_of(home_of(chip, across, row) * HEAD, HEAD), HEAD)
        start = 2 * index * HEAD
        out[:, start : start + HEAD] = key_weight[:, columns]
        out[:, start + HEAD : start + 2 * HEAD] = value_weight[:, columns]


def order_weights(key_weight, value_weight):
    features, depth = key_weight.shape
    outs = [((features, 2 * depth), BF)]
    return call("order_weights", order_body, outs, [key_weight, value_weight])[0]


def place_rows(place, left, mine, other):
    for half, pieces in ((place[0], mine), (1 - place[0], other)):
        rows = pl.ds(pl.multiple_of(half * HALF, HALF), HALF)
        chunks = [piece[row] for piece in pieces for row in range(piece.shape[0])]
        for index, chunk in enumerate(chunks):
            left[rows, 2 * index * HEAD : 2 * (index + 1) * HEAD] = chunk


def near_body(place, mine, mine_far, other, other_far, weight, out, left):
    place_rows(place, left, [mine, mine_far], [other, other_far])
    out[...] = contract_last(left[...], weight[:, : left.shape[1]])


def near_grads(place, mine, other, weight):
    features = weight.shape[0]
    scratch = [pltpu.VMEM((TOK, 6 * HEAD), BF)]
    outs = [((TOK, features), F32)]
    flops = 2 * TOK * features * 6 * HEAD
    args = [place, *mine, *other, weight]
    return call("near_grads", near_body, outs, args, scratch, 8, flops)[0]


def far_half(half, pieces, near, weight, columns):
    chunks = [piece[row] for piece in pieces for row in range(piece.shape[0])]
    left = jnp.concatenate(chunks, axis=1)
    rows = pl.ds(pl.multiple_of(half * HALF, HALF), HALF)
    right = weight[columns, weight.shape[1] - left.shape[1] :]
    return (near[rows, columns] + contract_last(left, right)).astype(BF)


def far_own_body(place, *refs):
    pieces, (near, weight, out) = refs[:-3], refs[-3:]
    steps = 4
    width = out.shape[1] // steps
    for step in range(steps):
        columns = pl.ds(step * width, width)
        out[:, columns] = far_half(place[0], pieces, near, weight, columns)


def far_own(place, pieces, near, weight):
    outs = [((HALF, weight.shape[0]), BF)]
    flops = 2 * HALF * weight.shape[0] * 10 * HEAD
    return call("far_own", far_own_body, outs, [place, *pieces, near, weight], (), 12, flops)[0]


def far_body(place, *refs):
    pieces, (own, near, weight, out, totals, sems) = refs[:-6], refs[-6:]
    own_rows, other_rows = [
        pl.ds(pl.multiple_of(half * HALF, HALF), HALF) for half in (place[0], 1 - place[0])
    ]
    steps, width = totals.shape[0], totals.shape[2]
    writes = [pltpu.make_async_copy(own, out.at[own_rows, :], sems.at[steps])]
    writes[0].start()
    for step in range(steps):
        columns = pl.ds(step * width, width)
        totals[step] = far_half(1 - place[0], pieces, near, weight, columns)
        target = out.at[other_rows, columns]
        writes.append(pltpu.make_async_copy(totals.at[step], target, sems.at[step]))
        writes[-1].start()
    for write in writes:
        write.wait()


def far_grads(place, pieces, own, near, weight):
    features = weight.shape[0]
    steps = 4
    scratch = [
        pltpu.VMEM((steps, HALF, features // steps), BF),
        pltpu.SemaphoreType.DMA((steps + 1,)),
    ]
    outs = [((TOK, features), BF)]
    args = [place, *pieces, own, near, weight]
    flops = 2 * HALF * features * 10 * HEAD
    return call("far_grads", far_body, outs, args, scratch, 12, flops, out_space=pltpu.HBM)[0]


def add_body(*refs):
    total = refs[0][...]
    for ref in refs[1:-1]:
        total = total + ref[...]
    refs[-1][...] = total


def add_up(*parts):
    return call("add_up", add_body, [(parts[0].shape, F32)], parts, mib=4)[0]


def pair_body(mine, other, out):
    out[0] = mine[...]
    out[1] = other[...]


def pair_up(mine, other):
    return call("pair", pair_body, [((2,) + mine.shape, BF)], [mine, other], mib=4)[0]


def own_core():
    return lax.rem(lax.axis_index("tensor"), 2)


def ring_body(here, direct, swapped, three, give):
    total = here[...] + direct[...]
    full = total + swapped[...]
    three[...] = full
    give[...] = jnp.where(own_core() == 0, full, total)


def ring_sums(*parts):
    return call("ring_sums", ring_body, [(parts[0].shape, F32)] * 2, parts, mib=4)


def ring_end_body(three, recv, out):
    out[...] = jnp.where(own_core() == 0, three[...], 0.0) + recv[...]


def ring_end(*parts):
    return call("ring_end", ring_end_body, [(parts[0].shape, F32)], parts, mib=4)[0]


def total_body(here, recv, key, value):
    total = here[...] + recv[...]
    own = lax.broadcasted_iota(jnp.int32, (NT, HEAD // 2), 1) >= 0
    own = own & (own_core() == 0)
    key[...] = jnp.where(own, total[:, : HEAD // 2], total[:, HEAD // 2 : HEAD])
    value[...] = jnp.where(own, total[:, HEAD : HEAD + HEAD // 2], total[:, HEAD + HEAD // 2 :])


def tenant_totals(here, recv):
    return pl.pallas_call(
        total_body,
        out_shape=[jax.ShapeDtypeStruct((NT, HEAD // 2), F32)] * 2,
        compiler_params=pltpu.CompilerParams(vmem_limit_bytes=4 * MIB),
        name="tenant_totals",
    )(here, recv)


def core_swap(array):
    return lax.ppermute(array, "tensor", CORE_SWAP)


def chip_from(array, across, row):
    if across == row == 0:
        return array
    pairs = tensor_pairs(lambda x, y, core: (x - across, y ^ row, core))
    return lax.ppermute(array, "tensor", pairs)


def depth_from(array, steps):
    pairs = []
    for z in range(8):
        for row in range(2):
            for chip in range(CHIPS):
                for core in range(2):
                    source = (z + steps[core]) % 8 * 2 + row
                    place = chip * 2 + core
                    pairs.append((source * 16 + place, (z * 2 + row) * 16 + place))
    return lax.ppermute(array, ("dp", "tensor"), pairs)


def on_device(
    tokens,
    queries,
    out_grad,
    key_weight,
    value_weight,
    key_scale,
    value_scale,
    segment_ids,
    tenant_ids,
):
    place = find_place(segment_ids, tenant_ids)
    key_send, tokens, key_weight, value_weight = load_project(tokens, key_weight, value_weight)
    key_recv = core_swap(key_send)
    value_send = project("project_value", True, tokens, [value_weight], [BF])[0]
    value_recv = core_swap(value_send)
    weights = [key_weight, value_weight]
    key_keep, value_keep = project("project_keep", False, tokens, weights, [F32, F32])
    sides = (key_keep, value_keep, key_recv, value_recv)
    part_21, part_11, part_31 = pack("pack_relayed", SENT[:3], *sides)
    part_10, part_30, kept_20, kept_01, kept_00 = pack("pack_rest", SENT[3:] + KEPT, *sides)
    part_20 = relay(kept_20, chip_from(part_21, 0, 1))
    part_01 = relay(kept_01, chip_from(part_11, -1, 0), chip_from(part_31, 1, 0))
    parts = [
        chip_from(part_10, -1, 0),
        chip_from(part_30, 1, 0),
        chip_from(part_20, 2, 0),
        chip_from(part_01, 0, 1),
    ]
    weight = order_weights(key_weight, value_weight)
    parts, weight, place = lax.optimization_barrier((parts, weight, place))
    base, low = finish(place, kept_00, *parts, key_scale, value_scale)
    low_other = core_swap(low)
    base_other = core_swap(base)
    send, keep = attention(place, low, low_other, queries, out_grad)
    recv = core_swap(send)
    sums = tenant_table(place, keep, send, base, base_other)
    recv, sums = lax.optimization_barrier((recv, sums))
    grad_low = scale_grads(place, keep, recv, key_scale, value_scale)
    grad_low, sums_other = lax.optimization_barrier((grad_low, core_swap(sums)))
    sums = add_up(sums, sums_other)
    row_part, ring = lax.optimization_barrier(
        (chip_from(grad_low, 0, 1), depth_from(sums, (-1, 1)))
    )
    pair, far_part = lax.optimization_barrier(
        (pair_up(grad_low, row_part), chip_from(grad_low, 2, 0))
    )
    three, give = ring_sums(sums, ring, core_swap(ring))
    early = [pair, far_part[None]]
    near = near_grads(place, early, [core_swap(piece) for piece in early], weight)
    arrived = [chip_from(pair, 1, 0), chip_from(pair, 3, 0), chip_from(far_part, 0, 1)]
    arrived, ring, near = lax.optimization_barrier((arrived, depth_from(give, (3, -3)), near))
    arrived = arrived[:2] + [arrived[2][None]]
    sums = ring_end(three, ring)
    own_half = far_own(place, arrived, near, weight)
    others, sums_other, own_half = lax.optimization_barrier(
        ([core_swap(piece) for piece in arrived], core_swap(sums), own_half)
    )
    sums = add_up(sums, sums_other)
    row_sums = lax.ppermute(sums, "dp", [(i, i ^ 1) for i in range(16)])
    input_grad = far_grads(place, others, own_half, near, weight)
    input_grad, row_sums = lax.optimization_barrier((input_grad, row_sums))
    key_total, value_total = tenant_totals(sums, row_sums)
    return input_grad, key_total, value_total


def solution(mesh):
    return jax.shard_map(
        on_device,
        mesh=mesh,
        in_specs=(
            P("dp", "tensor"),
            P("dp", "tensor"),
            P("dp", "tensor"),
            P("tensor", None),
            P("tensor", None),
            P(),
            P(),
            P("dp", None),
            P("dp", None),
        ),
        out_specs=(P("dp", "tensor"), P(None, "tensor"), P(None, "tensor")),
        check_vma=False,
    )
```
